256 devices in a mesh: tm: 64 (over x, z, y_hi), patch: 4 (over y_lo, core).
Axes of the slice: x: 4, y: 4 (y_hi: 2, y_lo: 2; y = y_hi * 2 + y_lo), z: 8, core: 2. Of those that a mesh axis runs over, the one named last changes fastest.
Arguments:
- frames_in: bfloat16 [1024, 196, 768], P('tm', 'patch'), may hold values from -12 to 12
- ln_time: float32 [768], replicated, may hold values from 0.25 to 1.75
- w_time_qkv: bfloat16 [768, 2304], replicated, may hold values from -2 to 2
- w_time_out: bfloat16 [768, 768], replicated, may hold values from -0.21875 to 0.21875
- ln_space: float32 [768], replicated, may hold values from 0.25 to 1.75
- w_space_qkv: bfloat16 [768, 2304], replicated, may hold values from -2 to 2
- w_space_out: bfloat16 [768, 768], replicated, may hold values from -0.21875 to 0.21875
- band_lo: int32 [64], P('tm'), may hold values from -1 to 0, as said below
- band_hi: int32 [64], P('tm'), may hold values from 0 to 1, as said below
- valid: int32 [64], replicated, may hold values from 0 to 1, as said below
Outputs:
- frames_out: bfloat16 [1024, 196, 768], P('tm', 'patch')
The draws below stay inside these ranges and needn't reach their ends.
Inputs may be any that keep to these rules, and one draw needn't show every extreme that they name: `band_lo`: every even-numbered block has -1, and so does block 1; block 3 has 0. `band_hi`: every even-numbered block has 1; block 3 has 0. `valid`: blocks 0 and 1 are 1; block 2 is 0.
All inputs are finite; a program needn't handle non-finite values.
Results may differ from the reference program's by a relative error of at most 0.009.
The reference program's roundings to bfloat16 on the way count: a program that leaves them out, or rounds other values in their place, can miss the bound.
Values may be sent and summed in bfloat16 or wider, within the bound.
A program may use at most 128 MiB of HBM per device.

```python
import jax
import jax.numpy as jnp
from jax import lax

D = 768
HEADS = 12
PATCHES = 196
BLOCK = 16
REACH = 1
BLK_DEV = 1
NBLK = 64
FRAMES = 1024


def draw_frames_in(key, part):
    key = jax.random.fold_in(key, 1)
    first = jax.random.fold_in(key, 0)
    values = jnp.clip(jax.random.normal(first, (FRAMES, PATCHES, D), jnp.float32), -6.0, 6.0)
    return values.astype(jnp.bfloat16)


def draw_w_time_qkv(key, part):
    key = jax.random.fold_in(key, 2)
    base = jnp.clip(jax.random.normal(key, (D, 3 * D), jnp.float32), -6.0, 6.0) * D ** (-0.5)
    values = base
    return values.astype(jnp.bfloat16)


def draw_w_space_qkv(key, part):
    key = jax.random.fold_in(key, 3)
    base = jnp.clip(jax.random.normal(key, (D, 3 * D), jnp.float32), -6.0, 6.0) * D ** (-0.5)
    values = base
    return values.astype(jnp.bfloat16)


def draw_band_lo(key, part):
    key = jax.random.fold_in(key, 5)
    values = jax.random.randint(key, (NBLK,), -REACH, 1, dtype=jnp.int32)
    blocks = jnp.arange(NBLK, dtype=jnp.int32)
    forced = (blocks // BLK_DEV % 2 == 0) & (blocks % BLK_DEV == 0)
    forced = forced | (blocks == BLK_DEV)
    values = jnp.where(forced, -REACH, values)
    return jnp.where(blocks == 3 * BLK_DEV, 0, values).astype(jnp.int32)


def draw_band_hi(key, part):
    key = jax.random.fold_in(key, 6)
    values = jax.random.randint(key, (NBLK,), 0, REACH + 1, dtype=jnp.int32)
    blocks = jnp.arange(NBLK, dtype=jnp.int32)
    forced = (blocks // BLK_DEV % 2 == 0) & (blocks % BLK_DEV == BLK_DEV - 1)
    values = jnp.where(forced, REACH, values)
    return jnp.where(blocks == 4 * BLK_DEV - 1, 0, values).astype(jnp.int32)


def draw_valid(key, part):
    key = jax.random.fold_in(key, 7)
    values = jax.random.randint(key, (NBLK,), 0, 2, dtype=jnp.int32)
    blocks = jnp.arange(NBLK, dtype=jnp.int32)
    kept = (blocks >= BLK_DEV - 1) & (blocks <= 2 * BLK_DEV - 1)
    values = jnp.where(kept, 1, values)
    return jnp.where(blocks == 2 * BLK_DEV, 0, values).astype(jnp.int32)


def bell_draw(rng, extent, scale, bound, kind=jnp.bfloat16):
    return jnp.clip(scale * jax.random.normal(rng, extent, jnp.float32), -bound, bound).astype(kind)


def setup_inputs(seed: int = 0) -> dict:
    key_list = jax.random.split(jax.random.key(seed), 11)
    frames_in = draw_frames_in(jax.random.fold_in(key_list[10], 71), 0)
    ln_time = jnp.clip(1.0 + 0.15 * jax.random.normal(key_list[1], (D,), jnp.float32), 0.25, 1.75)
    w_time_qkv = draw_w_time_qkv(jax.random.fold_in(key_list[10], 71), 0)
    w_time_out = bell_draw(key_list[3], (D, D), D ** -0.5, 0.21875)
    ln_space = jnp.clip(1.0 + 0.15 * jax.random.normal(key_list[4], (D,), jnp.float32), 0.25, 1.75)
    w_space_qkv = draw_w_space_qkv(jax.random.fold_in(key_list[10], 71), 0)
    w_space_out = bell_draw(key_list[6], (D, D), D ** -0.5, 0.21875)
    band_lo = draw_band_lo(jax.random.fold_in(key_list[10], 71), 0)
    band_hi = draw_band_hi(jax.random.fold_in(key_list[10], 71), 0)
    valid = draw_valid(jax.random.fold_in(key_list[10], 71), 0)
    return {"frames_in": frames_in, "ln_time": ln_time, "w_time_qkv": w_time_qkv, "w_time_out": w_time_out, "ln_space": ln_space, "w_space_qkv": w_space_qkv, "w_space_out": w_space_out, "band_lo": band_lo, "band_hi": band_hi, "valid": valid}


def layer_norm(values, gain):
    floats = values.astype(jnp.float32)
    center = floats - lax.optimization_barrier(jnp.mean(floats, axis=-1, keepdims=True))
    spread = lax.optimization_barrier(jnp.mean(center * center, axis=-1, keepdims=True))
    return (center * lax.rsqrt(spread + 1e-05) * gain).astype(jnp.bfloat16)

def soft_weights(scores):
    top = lax.optimization_barrier(jnp.max(scores, axis=-1, keepdims=True))
    raised = jnp.exp(scores - top)
    return (raised / lax.optimization_barrier(jnp.sum(raised, axis=-1, keepdims=True))).astype(jnp.bfloat16)

def split_heads(block):
    return block.astype(jnp.float32).reshape(block.shape[:-1] + (HEADS, block.shape[-1] // HEADS))

def reference(frames_in, ln_time, w_time_qkv, w_time_out, ln_space, w_space_qkv, w_space_out, band_lo, band_hi, valid):
    width = frames_in.shape[-1]
    scale = (width // HEADS) ** (-0.5)
    rim = REACH * BLOCK
    normed = layer_norm(frames_in, ln_time)
    packed = jnp.dot(normed.reshape(-1, width), w_time_qkv, preferred_element_type=jnp.float32)
    packed = packed.astype(jnp.bfloat16).reshape(FRAMES, PATCHES, 3 * width)
    query_all = packed[..., :width]
    padded = jnp.pad(packed[..., width:], ((rim, rim), (0, 0), (0, 0)))

    def temporal(block_id):
        query_rows = split_heads(lax.dynamic_slice_in_dim(query_all, block_id * BLOCK, BLOCK, 0))
        pairs = lax.dynamic_slice_in_dim(padded, block_id * BLOCK, BLOCK + 2 * rim, 0)
        key_rows = split_heads(pairs[..., :width])
        value_rows = split_heads(pairs[..., width:])
        scores = jnp.einsum('fphd,gphd->phfg', query_rows, key_rows) * scale
        key_block = block_id - REACH + jnp.arange(BLOCK + 2 * rim, dtype=jnp.int32) // BLOCK
        offset = key_block - block_id
        inside = (key_block >= 0) & (key_block < NBLK)
        marked = valid[jnp.clip(key_block, 0, NBLK - 1)] == 1
        allowed = (offset >= band_lo[block_id]) & (offset <= band_hi[block_id]) & inside & (marked | (offset == 0))
        scores = jnp.where(allowed, scores, -jnp.inf)
        weights = soft_weights(scores)
        mixed = jnp.einsum('phfg,gphd->fphd', weights.astype(jnp.float32), value_rows)
        return mixed.astype(jnp.bfloat16).reshape(BLOCK, PATCHES, width)
    attended = lax.map(temporal, jnp.arange(NBLK, dtype=jnp.int32)).reshape(-1, width)
    after_time = frames_in.astype(jnp.float32).reshape(-1, width) + jnp.dot(attended, w_time_out, preferred_element_type=jnp.float32)
    after_time = after_time.astype(jnp.bfloat16).reshape(FRAMES, PATCHES, width)
    normed = layer_norm(after_time, ln_space)
    packed = jnp.dot(normed.reshape(-1, width), w_space_qkv, preferred_element_type=jnp.float32)
    packed = packed.astype(jnp.bfloat16).reshape(FRAMES, PATCHES, 3 * width)

    def spatial(frame):
        query_rows = split_heads(frame[:, :width])
        key_rows = split_heads(frame[:, width:2 * width])
        value_rows = split_heads(frame[:, 2 * width:])
        scores = jnp.einsum('phd,qhd->hpq', query_rows, key_rows) * scale
        weights = soft_weights(scores)
        mixed = jnp.einsum('hpq,qhd->phd', weights.astype(jnp.float32), value_rows)
        return mixed.astype(jnp.bfloat16).reshape(PATCHES, width)
    attended = lax.map(spatial, packed).reshape(-1, width)
    result = after_time.astype(jnp.float32).reshape(-1, width) + jnp.dot(attended, w_space_out, preferred_element_type=jnp.float32)
    return result.astype(jnp.bfloat16).reshape(FRAMES, PATCHES, width)
```

```python
import functools

import jax
import jax.numpy as jnp
from jax import lax
from jax.experimental import pallas as pl
from jax.experimental.pallas import tpu as pltpu
from jax.sharding import PartitionSpec as P

MESH = pl.DeviceIdType.MESH
F32 = jnp.float32
BF16 = jnp.bfloat16
HEADS = 12
BLOCK = 16
WIDTH = 768
PATCH = 49
HALF = 25
GROUP = 8
CHUNKS = 3
BOUNDS = (0, 9, 17, 25)
TOKENS = 208
VALID = 196
NT = (((1,), (1,)), ((), ()))
NINF = float("-inf")


def dot(a, b):
    return jnp.dot(a, b, preferred_element_type=F32)


def norm_rows(values, gain):
    floats = values.astype(F32)
    center = floats - jnp.mean(floats, axis=-1, keepdims=True)
    spread = jnp.mean(center * center, axis=-1, keepdims=True)
    return (center * lax.rsqrt(spread + 1e-05) * gain).astype(BF16)


def select_matrix(rows, cols, source):
    row = lax.broadcasted_iota(jnp.int32, (rows, cols), 0)
    col = lax.broadcasted_iota(jnp.int32, (rows, cols), 1)
    return jnp.where(source(row) == col, 1.0, 0.0).astype(BF16)


def bits(value, low, count):
    return (value >> low) & ((1 << count) - 1)


def cols_of(j, base=0):
    return pl.ds(pl.multiple_of(base + j * 256, 256), 256)


def kernel(
    x_hbm, wtq_hbm, wto_hbm, wsq_hbm, wso_hbm, gain_t, gain_s, band_lo, band_hi, valid, out,
    wtq, wto, wsq, wso, x4, nrm, kv, qs, mix, snd, lft, recv, rcl, xs, nrm2, qkv, smix,
    om, ol, ret, rl, retl, biasb, bias, perm1, perm2, perm3, perm5,
    lsem, csem, psnd, prcv, osnd, orcv, rsnd, rrcv, bsem,
    ssnd, srcv, lsnd, lrcv, tsnd, trcv, usnd, urcv,
):
    tm = lax.axis_index("tm")
    me = lax.axis_index("patch")
    pairs = lax.axis_size("tm") // 2
    pair = tm // 2
    side = tm % 2
    own = 1 + side
    other = 2 - side
    gid = side * 4 + me
    out_pair = (pair + 2 * side - 1 + pairs) % pairs
    rly_pair = (pair + 1 - 2 * side + pairs) % pairs
    partner = (pair * 2 + 1 - side, me)
    out_dev = (out_pair * 2 + side, me)
    rly_dev = (rly_pair * 2 + side, me)

    def member(k):
        d = (gid + k) % 8
        return d, (pair * 2 + d // 4, d % 4)

    def peer(k):
        s = (me + k) % 4
        return s, (tm, s)

    def remote(src, dst, snd_sem, rcv_sem, device):
        return pltpu.make_async_remote_copy(
            src_ref=src, dst_ref=dst, send_sem=snd_sem, recv_sem=rcv_sem,
            device_id=device, device_id_type=MESH,
        )

    own_copy = pltpu.make_async_copy(x_hbm.at[pl.ds(24 * side, HALF)], x4.at[own], lsem.at[0])
    own_copy.start()
    w_copies = []
    for i, (src, dst) in enumerate(((wtq_hbm, wtq), (wto_hbm, wto), (wsq_hbm, wsq), (wso_hbm, wso))):
        cp = pltpu.make_async_copy(src, dst, lsem.at[1 + i])
        cp.start()
        w_copies.append(cp)

    barrier = pltpu.get_barrier_semaphore()
    for k in range(1, 8):
        pl.semaphore_signal(barrier, inc=1, device_id=member(k)[1], device_id_type=MESH)
    pl.semaphore_signal(barrier, inc=1, device_id=out_dev, device_id_type=MESH)
    pl.semaphore_signal(barrier, inc=1, device_id=rly_dev, device_id_type=MESH)
    pl.semaphore_wait(barrier, 9)

    part, outer = [], []
    for c in range(CHUNKS):
        lo, n = BOUNDS[c], BOUNDS[c + 1] - BOUNDS[c]
        part.append(remote(
            x_hbm.at[pl.ds(24 * (1 - side) + lo, n)], x4.at[own, pl.ds(lo, n)],
            psnd.at[c], prcv.at[c], partner,
        ))
        outer.append(remote(
            x_hbm.at[pl.ds(24 * side + lo, n)], x4.at[3 - 3 * side, pl.ds(lo, n)],
            osnd.at[c], orcv.at[c], out_dev,
        ))
    relay = []
    for c in range(CHUNKS):
        lo, n = BOUNDS[c], BOUNDS[c + 1] - BOUNDS[c]
        relay.append(remote(
            x4.at[other, pl.ds(lo, n)], x4.at[3 * side, pl.ds(lo, n)],
            rsnd.at[c], rrcv.at[c], rly_dev,
        ))
    for c in range(CHUNKS):
        part[c].start()
        outer[c].start()

    left_ok = (band_lo[0] <= -1) & (tm >= 1) & (valid[jnp.maximum(tm - 1, 0)] == 1)
    right_ok = (band_hi[0] >= 1) & (tm <= 2 * pairs - 2) & (valid[jnp.minimum(tm + 1, 2 * pairs - 1)] == 1)
    left = jnp.where(left_ok, 0.0, NINF)
    right = jnp.where(right_ok, 0.0, NINF)
    row8 = lax.broadcasted_iota(jnp.int32, (8, 128), 0)
    biasb[side] = jnp.where(row8 == 0, left, right)
    bias_copy = remote(biasb.at[side], biasb.at[side], bsem.at[0], bsem.at[1], partner)
    bias_copy.start()

    perm1[...] = select_matrix(128, 128, lambda r: (bits(r, 2, 3) << 4) | (bits(r, 5, 2) << 2) | bits(r, 0, 2))
    perm2[...] = select_matrix(
        256, 256,
        lambda r: (bits(r, 3, 1) << 7) | (bits(r, 4, 2) << 5) | (bits(r, 0, 3) << 2) | bits(r, 6, 2),
    )
    perm5[...] = select_matrix(256, 256, lambda r: (bits(r, 0, 4) << 4) | bits(r, 4, 4))
    perm3[0] = select_matrix(
        64, 64, lambda r: jnp.where(bits(r, 0, 4) < 4, (bits(r, 0, 2) << 4) + me * 4 + bits(r, 4, 2), -1)
    )
    perm3[1] = select_matrix(
        64, 64, lambda r: jnp.where(bits(r, 2, 2) == me, (bits(r, 0, 2) << 4) + bits(r, 4, 2), -1)
    )

    lane256 = lax.broadcasted_iota(jnp.int32, (1, 256), 1) >> 6
    head_f = [lane256 == h for h in range(4)]
    head_b = [jnp.where(m, 1.0, 0.0).astype(BF16) for m in head_f]

    bias_copy.wait()
    key_slot = lax.broadcasted_iota(jnp.int32, (32, 64), 1) >> 4
    query_blk = lax.broadcasted_iota(jnp.int32, (32, 64), 0) >> 4
    offset = key_slot - 1 - query_blk
    one = jnp.where(
        query_blk == 0,
        jnp.where(offset < 0, biasb[0, 0:1, 0:64], biasb[0, 1:2, 0:64]),
        jnp.where(offset < 0, biasb[1, 0:1, 0:64], biasb[1, 1:2, 0:64]),
    )
    one = jnp.where(offset == 0, 0.0, one)
    one = jnp.where((offset > 1) | (offset < -1), NINF, one)
    for h in range(4):
        bias[32 * h:32 * h + 32] = one

    def attend(k_rows, q_rows, m_rows):
        q_all = [qs[pl.ds(r, 16)] for r in q_rows]
        for g in range(3):
            cols = slice(256 * g, 256 * g + 256)
            vcols = slice(768 + 256 * g, 768 + 256 * g + 256)
            keys = jnp.concatenate([kv[pl.ds(r, 16), cols] for r in k_rows], axis=0)
            vals = jnp.concatenate([kv[pl.ds(r, 16), vcols] for r in k_rows], axis=0)
            query = jnp.concatenate([q[:, cols] for q in q_all], axis=0)
            stacked = jnp.concatenate([query * m for m in head_b], axis=0)
            score = lax.dot_general(stacked, keys, NT, preferred_element_type=F32) + bias[...]
            raised = jnp.exp(score - jnp.max(score, axis=-1, keepdims=True))
            total = jnp.sum(raised, axis=-1, keepdims=True)
            weight = (raised * (1.0 / total)).astype(BF16)
            mixed = dot(weight, vals)
            picked = jnp.where(head_f[0], mixed[0:32], 0.0)
            for h in range(1, 4):
                picked = jnp.where(head_f[h], mixed[32 * h:32 * h + 32], picked)
            picked = picked.astype(BF16)
            mix[pl.ds(m_rows[0], 16), cols] = picked[:16]
            mix[pl.ds(m_rows[1], 16), cols] = picked[16:]

    lo_at = 24 - 24 * side

    def temporal(c):
        last = c == CHUNKS - 1
        s0 = side + GROUP * c
        main = (0, 128, 256, 416 if last else 384)
        extra = (544, 384, 400, 560)
        rows = 576 if last else 512
        q_rows = 288 if last else 256
        for slot in range(4):
            for half in range(2):
                block = x4[slot, pl.ds(s0 + 4 * half, 4)].reshape(64, WIDTH)
                nrm[main[slot] + 64 * half:main[slot] + 64 * half + 64] = norm_rows(block, gain_t[...])
            if last:
                nrm[extra[slot]:extra[slot] + 16] = norm_rows(x4[slot, lo_at], gain_t[...])

        def kv_tile(j, _):
            kv[0:rows, cols_of(j)] = dot(nrm[0:rows], wtq[:, cols_of(j, WIDTH)]).astype(BF16)
            return 0

        def q_tile(j, _):
            tile = dot(nrm[128:128 + q_rows], wtq[:, cols_of(j)]).astype(BF16)
            qs[0:q_rows, cols_of(j)] = tile * jnp.asarray(0.125, BF16)
            return 0

        lax.fori_loop(0, 6, kv_tile, 0)
        lax.fori_loop(0, 3, q_tile, 0)

        def step(i, _):
            for u in range(2):
                at = pl.multiple_of((2 * i + u) * 16, 16)
                attend([pl.multiple_of(m + at, 16) for m in main],
                       [at, pl.multiple_of(128 + at, 16)], [at, pl.multiple_of(128 + at, 16)])
            return 0

        lax.fori_loop(0, GROUP // 2, step, 0)
        if last:
            attend(list(extra), [256, 272], [256, 272])

        def out_tile(j, _):
            cols = cols_of(j)
            acc = dot(mix[0:q_rows], wto[:, cols])
            base = x4[1:3, pl.ds(s0, GROUP), :, cols].reshape(256, 256)
            after = (base.astype(F32) + acc[0:256]).astype(BF16)
            for b in range(2):
                moved = dot(perm1[...], after[128 * b:128 * b + 128]).astype(BF16)
                snd[c, 4 * b:4 * b + 4, :, cols] = moved.reshape(4, 32, 256)
            if last:
                base = x4[1:3, lo_at, :, cols].reshape(32, 256)
                lft[:, :, cols] = (base.astype(F32) + acc[256:288]).astype(BF16).reshape(2, 16, 256)
            return 0

        lax.fori_loop(0, 3, out_tile, 0)

    def scatter(c):
        copies = []
        pltpu.make_async_copy(snd.at[c, gid], recv.at[c, gid], csem.at[c]).start()
        for k in range(1, 8):
            d, device = member(k)
            cp = remote(snd.at[c, d], recv.at[c, gid], ssnd.at[c, k], srcv.at[c, k], device)
            cp.start()
            copies.append(cp)
        return copies

    own_copy.wait()
    part[0].wait_recv()
    relay[0].start()
    part[1].wait_recv()
    relay[1].start()
    w_copies[0].wait()
    w_copies[1].wait()
    scattered = []
    for c in range(CHUNKS):
        outer[c].wait_recv()
        relay[c].wait_recv()
        temporal(c)
        scattered.append(scatter(c))
        if c == 0:
            part[2].wait_recv()
            relay[2].start()
    left_copies = []
    pltpu.make_async_copy(lft.at[side], rcl.at[me], csem.at[3]).start()
    for k in range(1, 4):
        s, device = peer(k)
        cp = remote(lft.at[side], rcl.at[me], lsnd.at[k], lrcv.at[k], device)
        cp.start()
        left_copies.append(cp)
    w_copies[2].wait()
    w_copies[3].wait()

    def gather(c):
        last = c == CHUNKS - 1
        pltpu.make_async_copy(snd.at[c, gid], recv.at[c, gid], csem.at[c]).wait()
        for cp in scattered[c]:
            cp.wait_recv()
        rows = 320 if last else 256

        def move(j, _):
            cols = cols_of(j)
            moved = dot(perm2[...], recv[c, :, :, cols].reshape(256, 256)).astype(BF16)
            xs[:, 64 * c:64 * c + 64, cols] = moved.reshape(4, 64, 256)
            return 0

        lax.fori_loop(0, 3, move, 0)
        if last:
            pltpu.make_async_copy(lft.at[side], rcl.at[me], csem.at[3]).wait()
            for cp in left_copies:
                cp.wait_recv()

            def move_left(j, _):
                cols = cols_of(j)
                moved = dot(perm3[0], rcl[:, :, cols].reshape(64, 256)).astype(BF16)
                xs[:, 192:208, cols] = moved.reshape(4, 16, 256)
                return 0

            lax.fori_loop(0, 3, move_left, 0)
        for f in range(4):
            nrm2[64 * f:64 * f + 64] = norm_rows(xs[f, 64 * c:64 * c + 64], gain_s[...])
        if last:
            nrm2[256:320] = norm_rows(xs[:, 192:208].reshape(64, WIDTH), gain_s[...])

        def put(tile, cols):
            qkv[:, 64 * c:64 * c + 64, cols] = tile[0:256].reshape(4, 64, 256)
            if last:
                qkv[:, 192:208, cols] = tile[256:320].reshape(4, 16, 256)

        def q_tile(j, _):
            tile = dot(nrm2[0:rows], wsq[:, cols_of(j)]).astype(BF16)
            put(tile * jnp.asarray(0.125, BF16), cols_of(j))
            return 0

        def kv_tile(j, _):
            put(dot(nrm2[0:rows], wsq[:, cols_of(j)]).astype(BF16), cols_of(j))
            return 0

        lax.fori_loop(0, 3, q_tile, 0)
        lax.fori_loop(3, 9, kv_tile, 0)

    for c in range(CHUNKS):
        gather(c)

    lane128 = lax.broadcasted_iota(jnp.int32, (1, 128), 1)
    low = lane128 < 64
    low_b = jnp.where(low, 1.0, 0.0).astype(BF16)
    high_b = jnp.where(low, 0.0, 1.0).astype(BF16)
    key_ok = lax.broadcasted_iota(jnp.int32, (1, TOKENS), 1) < VALID

    def frame(f, _):
        def heads(j, _):
            cols = pl.ds(pl.multiple_of(j * 128, 128), 128)
            query = qkv[f, :, cols]
            keys = qkv[f, :, pl.ds(pl.multiple_of(WIDTH + j * 128, 128), 128)]
            vals = qkv[f, :, pl.ds(pl.multiple_of(2 * WIDTH + j * 128, 128), 128)]
            parts = []
            for mine, rest in ((low_b, high_b), (high_b, low_b)):
                score = lax.dot_general(query * mine, keys, NT, preferred_element_type=F32)
                score = jnp.where(key_ok, score, NINF)
                raised = jnp.exp(score - jnp.max(score, axis=-1, keepdims=True)).astype(BF16)
                parts.append(dot(raised, vals * mine + rest))
            top = jnp.where(low, parts[0], parts[1])
            total = pltpu.roll(jnp.where(low, parts[1], parts[0]), 64, 1)
            smix[:, cols] = (top / total).astype(BF16)
            return 0

        lax.fori_loop(0, 6, heads, 0)

        def out_tile(j, _):
            cols = cols_of(j)
            done = (xs[f, :, cols].astype(F32) + dot(smix[...], wso[:, cols])).astype(BF16)
            om[f, :, :, :, cols] = done[0:192].reshape(3, 4, 16, 256)
            ol[f, :, cols] = done[192:208]
            return 0

        lax.fori_loop(0, 3, out_tile, 0)
        pltpu.make_async_copy(om.at[f, :, me], ret.at[4 * me + f], tsnd.at[f, 0]).start()
        for k in range(1, 4):
            s, device = peer(k)
            remote(om.at[f, :, s], ret.at[4 * me + f], tsnd.at[f, k], trcv.at[f, k], device).start()
        return 0

    lax.fori_loop(0, 4, frame, 0)

    def spread(j, _):
        cols = cols_of(j)
        rl[:, :, cols] = dot(perm3[1], ol[:, :, cols].reshape(64, 256)).astype(BF16).reshape(4, 16, 256)
        return 0

    lax.fori_loop(0, 3, spread, 0)
    pltpu.make_async_copy(rl.at[me], retl.at[me], usnd.at[0]).start()
    for k in range(1, 4):
        s, device = peer(k)
        remote(rl.at[s], retl.at[me], usnd.at[k], urcv.at[k], device).start()

    for f in range(4):
        pltpu.make_async_copy(om.at[f, :, me], ret.at[4 * me + f], tsnd.at[f, 0]).wait()
        for k in range(1, 4):
            s, device = peer(k)
            remote(om.at[f, :, s], ret.at[4 * me + f], tsnd.at[f, k], trcv.at[f, k], device).wait()

    def finish(j, _):
        cols = cols_of(j)
        for c in range(CHUNKS):
            moved = dot(perm5[...], ret[:, c, :, cols].reshape(256, 256)).astype(BF16).reshape(16, 16, 256)
            out[8 * c:8 * c + 8, :, cols] = moved[0:8]
            out[25 + 8 * c:33 + 8 * c, :, cols] = moved[8:16]
        return 0

    lax.fori_loop(0, 3, finish, 0)
    pltpu.make_async_copy(rl.at[me], retl.at[me], usnd.at[0]).wait()
    for k in range(1, 4):
        s, device = peer(k)
        remote(rl.at[s], retl.at[me], usnd.at[k], urcv.at[k], device).wait()
    out[24] = (retl[0] + retl[1]) + (retl[2] + retl[3])

    for c in range(CHUNKS):
        part[c].wait_send()
        outer[c].wait_send()
        relay[c].wait_send()
        for cp in scattered[c]:
            cp.wait_send()
    for cp in left_copies:
        cp.wait_send()


def on_device(frames_in, ln_time, w_time_qkv, w_time_out, ln_space, w_space_qkv, w_space_out, band_lo, band_hi, valid):
    x = jnp.transpose(frames_in, (1, 0, 2))
    any_spec = pl.BlockSpec(memory_space=pl.ANY)
    vmem_spec = pl.BlockSpec(memory_space=pltpu.VMEM)
    smem_spec = pl.BlockSpec(memory_space=pltpu.SMEM)
    dma = pltpu.SemaphoreType.DMA
    scratch = [
        pltpu.VMEM((WIDTH, 3 * WIDTH), BF16),
        pltpu.VMEM((WIDTH, WIDTH), BF16),
        pltpu.VMEM((WIDTH, 3 * WIDTH), BF16),
        pltpu.VMEM((WIDTH, WIDTH), BF16),
        pltpu.VMEM((4, HALF, BLOCK, WIDTH), BF16),
        pltpu.VMEM((576, WIDTH), BF16),
        pltpu.VMEM((576, 2 * WIDTH), BF16),
        pltpu.VMEM((288, WIDTH), BF16),
        pltpu.VMEM((288, WIDTH), BF16),
        pltpu.VMEM((CHUNKS, 8, 32, WIDTH), BF16),
        pltpu.VMEM((2, BLOCK, WIDTH), BF16),
        pltpu.VMEM((CHUNKS, 8, 32, WIDTH), BF16),
        pltpu.VMEM((4, BLOCK, WIDTH), BF16),
        pltpu.VMEM((4, TOKENS, WIDTH), BF16),
        pltpu.VMEM((320, WIDTH), BF16),
        pltpu.VMEM((4, TOKENS, 3 * WIDTH), BF16),
        pltpu.VMEM((TOKENS, WIDTH), BF16),
        pltpu.VMEM((4, CHUNKS, 4, BLOCK, WIDTH), BF16),
        pltpu.VMEM((4, BLOCK, WIDTH), BF16),
        pltpu.VMEM((BLOCK, CHUNKS, BLOCK, WIDTH), BF16),
        pltpu.VMEM((4, BLOCK, WIDTH), BF16),
        pltpu.VMEM((4, BLOCK, WIDTH), BF16),
        pltpu.VMEM((2, 8, 128), F32),
        pltpu.VMEM((128, 64), F32),
        pltpu.VMEM((128, 128), BF16),
        pltpu.VMEM((256, 256), BF16),
        pltpu.VMEM((2, 64, 64), BF16),
        pltpu.VMEM((256, 256), BF16),
        dma((5,)), dma((4,)),
        dma((3,)), dma((3,)), dma((3,)), dma((3,)), dma((3,)), dma((3,)), dma((2,)),
        dma((3, 8)), dma((3, 8)), dma((4,)), dma((4,)),
        dma((4, 4)), dma((4, 4)), dma((4,)), dma((4,)),
    ]
    result = pl.pallas_call(
        kernel,
        out_shape=jax.ShapeDtypeStruct((PATCH, BLOCK, WIDTH), BF16),
        in_specs=[any_spec] * 5 + [vmem_spec] * 2 + [smem_spec] * 3,
        out_specs=vmem_spec,
        scratch_shapes=scratch,
        compiler_params=pltpu.CompilerParams(
            collective_id=0, has_side_effects=True, vmem_limit_bytes=56 * 1024 * 1024
        ),
    )(
        x, w_time_qkv, w_time_out, w_space_qkv, w_space_out,
        ln_time.reshape(1, WIDTH), ln_space.reshape(1, WIDTH), band_lo, band_hi, valid,
    )
    return jnp.transpose(result, (1, 0, 2))


def solution(mesh):
    placed = (P("tm", "patch", None), P(), P(), P(), P(), P(), P(), P("tm"), P("tm"), P())
    return jax.shard_map(
        on_device, mesh=mesh, in_specs=placed, out_specs=P("tm", "patch", None), check_vma=False
    )
```

```python
import functools

import jax
import jax.numpy as jnp
from jax import lax
from jax.experimental import pallas as pl
from jax.experimental.pallas import tpu as pltpu
from jax.sharding import PartitionSpec as P

MESH = pl.DeviceIdType.MESH
F32 = jnp.float32
BF16 = jnp.bfloat16
HEADS = 12
BLOCK = 16
WIDTH = 768
PATCH = 49
HALF = 25
GROUP = 8
CHUNKS = 3
BOUNDS = (0, 9, 17, 25)
TOKENS = 208
VALID = 196
NT = (((1,), (1,)), ((), ()))
NINF = float("-inf")


def dot(a, b):
    return jnp.dot(a, b, preferred_element_type=F32)


def norm_rows(values, gain):
    floats = values.astype(F32)
    center = floats - jnp.mean(floats, axis=-1, keepdims=True)
    spread = jnp.mean(center * center, axis=-1, keepdims=True)
    return (center * lax.rsqrt(spread + 1e-05) * gain).astype(BF16)


def select_matrix(rows, cols, source):
    row = lax.broadcasted_iota(jnp.int32, (rows, cols), 0)
    col = lax.broadcasted_iota(jnp.int32, (rows, cols), 1)
    return jnp.where(source(row) == col, 1.0, 0.0).astype(BF16)


def bits(value, low, count):
    return (value >> low) & ((1 << count) - 1)


def kernel(
    x_hbm, wtq_hbm, wto_hbm, wsq_hbm, wso_hbm, gain_t, gain_s, band_lo, band_hi, valid, out,
    wtq, wto, wsq, wso, x4, nrm, kv, qs, mix, snd, lft, recv, rcl, xs, nrm2, qkv, smix,
    om, ol, ret, rl, retl, biasb, bias, perm1, perm2, perm3, perm5,
    lsem, csem, psnd, prcv, osnd, orcv, rsnd, rrcv, bsem,
    ssnd, srcv, lsnd, lrcv, tsnd, trcv, usnd, urcv,
):
    tm = lax.axis_index("tm")
    me = lax.axis_index("patch")
    pairs = lax.axis_size("tm") // 2
    pair = tm // 2
    side = tm % 2
    own = 1 + side
    other = 2 - side
    gid = side * 4 + me
    out_pair = (pair + 2 * side - 1 + pairs) % pairs
    rly_pair = (pair + 1 - 2 * side + pairs) % pairs
    partner = (pair * 2 + 1 - side, me)
    out_dev = (out_pair * 2 + side, me)
    rly_dev = (rly_pair * 2 + side, me)

    def member(k):
        d = (gid + k) % 8
        return d, (pair * 2 + d // 4, d % 4)

    def peer(k):
        s = (me + k) % 4
        return s, (tm, s)

    def remote(src, dst, snd_sem, rcv_sem, device):
        return pltpu.make_async_remote_copy(
            src_ref=src, dst_ref=dst, send_sem=snd_sem, recv_sem=rcv_sem,
            device_id=device, device_id_type=MESH,
        )

    own_copy = pltpu.make_async_copy(x_hbm.at[pl.ds(24 * side, HALF)], x4.at[own], lsem.at[0])
    own_copy.start()
    w_copies = []
    for i, (src, dst) in enumerate(((wtq_hbm, wtq), (wto_hbm, wto), (wsq_hbm, wsq), (wso_hbm, wso))):
        cp = pltpu.make_async_copy(src, dst, lsem.at[1 + i])
        cp.start()
        w_copies.append(cp)

    barrier = pltpu.get_barrier_semaphore()
    for k in range(1, 8):
        pl.semaphore_signal(barrier, inc=1, device_id=member(k)[1], device_id_type=MESH)
    pl.semaphore_signal(barrier, inc=1, device_id=out_dev, device_id_type=MESH)
    pl.semaphore_signal(barrier, inc=1, device_id=rly_dev, device_id_type=MESH)
    pl.semaphore_wait(barrier, 9)

    part, outer = [], []
    for c in range(CHUNKS):
        lo, n = BOUNDS[c], BOUNDS[c + 1] - BOUNDS[c]
        part.append(remote(
            x_hbm.at[pl.ds(24 * (1 - side) + lo, n)], x4.at[own, pl.ds(lo, n)],
            psnd.at[c], prcv.at[c], partner,
        ))
        outer.append(remote(
            x_hbm.at[pl.ds(24 * side + lo, n)], x4.at[3 - 3 * side, pl.ds(lo, n)],
            osnd.at[c], orcv.at[c], out_dev,
        ))
    relay = []
    for c in range(CHUNKS):
        lo, n = BOUNDS[c], BOUNDS[c + 1] - BOUNDS[c]
        relay.append(remote(
            x4.at[other, pl.ds(lo, n)], x4.at[3 * side, pl.ds(lo, n)],
            rsnd.at[c], rrcv.at[c], rly_dev,
        ))
    for c in range(CHUNKS):
        part[c].start()
        outer[c].start()

    left_ok = (band_lo[0] <= -1) & (tm >= 1) & (valid[jnp.maximum(tm - 1, 0)] == 1)
    right_ok = (band_hi[0] >= 1) & (tm <= 2 * pairs - 2) & (valid[jnp.minimum(tm + 1, 2 * pairs - 1)] == 1)
    left = jnp.where(left_ok, 0.0, NINF)
    right = jnp.where(right_ok, 0.0, NINF)
    row8 = lax.broadcasted_iota(jnp.int32, (8, 128), 0)
    biasb[side] = jnp.where(row8 == 0, left, right)
    bias_copy = remote(biasb.at[side], biasb.at[side], bsem.at[0], bsem.at[1], partner)
    bias_copy.start()

    perm1[...] = select_matrix(128, 128, lambda r: (bits(r, 2, 3) << 4) | (bits(r, 5, 2) << 2) | bits(r, 0, 2))
    perm2[...] = select_matrix(
        256, 256,
        lambda r: (bits(r, 3, 1) << 7) | (bits(r, 4, 2) << 5) | (bits(r, 0, 3) << 2) | bits(r, 6, 2),
    )
    perm5[...] = select_matrix(256, 256, lambda r: (bits(r, 0, 4) << 4) | bits(r, 4, 4))
    perm3[0] = select_matrix(
        64, 64, lambda r: jnp.where(bits(r, 0, 4) < 4, (bits(r, 0, 2) << 4) + me * 4 + bits(r, 4, 2), -1)
    )
    perm3[1] = select_matrix(
        64, 64, lambda r: jnp.where(bits(r, 2, 2) == me, (bits(r, 0, 2) << 4) + bits(r, 4, 2), -1)
    )

    lane256 = lax.broadcasted_iota(jnp.int32, (1, 256), 1) >> 6
    head_f = [lane256 == h for h in range(4)]
    head_b = [jnp.where(m, 1.0, 0.0).astype(BF16) for m in head_f]

    bias_copy.wait()
    key_slot = lax.broadcasted_iota(jnp.int32, (32, 64), 1) >> 4
    query_blk = lax.broadcasted_iota(jnp.int32, (32, 64), 0) >> 4
    offset = key_slot - 1 - query_blk
    one = jnp.where(
        query_blk == 0,
        jnp.where(offset < 0, biasb[0, 0:1, 0:64], biasb[0, 1:2, 0:64]),
        jnp.where(offset < 0, biasb[1, 0:1, 0:64], biasb[1, 1:2, 0:64]),
    )
    one = jnp.where(offset == 0, 0.0, one)
    one = jnp.where((offset > 1) | (offset < -1), NINF, one)
    for h in range(4):
        bias[32 * h:32 * h + 32] = one

    def project(slots, lo, n, queries):
        rows = 16 * n
        for i, slot in enumerate(slots):
            block = x4[slot, lo:lo + n].reshape(rows, WIDTH)
            nrm[rows * i:rows * i + rows] = norm_rows(block, gain_t[...].reshape(1, WIDTH))
        normed = nrm[0:rows * len(slots)]
        pairs_kv = dot(normed, wtq[:, WIDTH:]).astype(BF16)
        for i, slot in enumerate(slots):
            kv[slot, 16 * lo:16 * lo + rows] = pairs_kv[rows * i:rows * i + rows]
        if queries:
            query = dot(normed, wtq[:, 0:WIDTH]).astype(BF16) * jnp.asarray(0.125, BF16)
            qs[slots[0] - 1, 16 * lo:16 * lo + rows] = query

    def attend(at, m_rows):
        q_all = [qs[b, pl.ds(at, 16)] for b in range(2)]
        for g in range(3):
            cols = slice(256 * g, 256 * g + 256)
            vcols = slice(768 + 256 * g, 768 + 256 * g + 256)
            keys = jnp.concatenate([kv[slot, pl.ds(at, 16), cols] for slot in range(4)], axis=0)
            vals = jnp.concatenate([kv[slot, pl.ds(at, 16), vcols] for slot in range(4)], axis=0)
            query = jnp.concatenate([q[:, cols] for q in q_all], axis=0)
            stacked = jnp.concatenate([query * m for m in head_b], axis=0)
            score = lax.dot_general(stacked, keys, NT, preferred_element_type=F32) + bias[...]
            raised = jnp.exp(score - jnp.max(score, axis=-1, keepdims=True))
            total = jnp.sum(raised, axis=-1, keepdims=True)
            weight = (raised * (1.0 / total)).astype(BF16)
            mixed = dot(weight, vals)
            picked = jnp.where(head_f[0], mixed[0:32], 0.0)
            for h in range(1, 4):
                picked = jnp.where(head_f[h], mixed[32 * h:32 * h + 32], picked)
            picked = picked.astype(BF16)
            mix[m_rows[0]:m_rows[0] + 16, cols] = picked[:16]
            mix[m_rows[1]:m_rows[1] + 16, cols] = picked[16:]

    lo_at = 24 - 24 * side

    def temporal(c):
        last = c == CHUNKS - 1
        s0 = side + GROUP * c
        for j in range(GROUP):
            attend(pl.multiple_of((s0 + j) * 16, 16), (16 * j, 128 + 16 * j))
        if last:
            attend(pl.multiple_of(lo_at * 16, 16), (256, 272))
        acc = dot(mix[0:288 if last else 256], wto[...])
        base = x4[1:3, pl.ds(s0, GROUP)].reshape(256, WIDTH)
        after = (base.astype(F32) + acc[0:256]).astype(BF16)
        for b in range(2):
            moved = dot(perm1[...], after[128 * b:128 * b + 128]).astype(BF16)
            snd[c, 4 * b:4 * b + 4] = moved.reshape(4, 32, WIDTH)
        if last:
            base = x4[1:3, lo_at].reshape(32, WIDTH)
            lft[...] = (base.astype(F32) + acc[256:288]).astype(BF16).reshape(2, 16, WIDTH)

    def scatter(c):
        copies = []
        pltpu.make_async_copy(snd.at[c, gid], recv.at[c, gid], csem.at[c]).start()
        for k in range(1, 8):
            d, device = member(k)
            cp = remote(snd.at[c, d], recv.at[c, gid], ssnd.at[c, k], srcv.at[c, k], device)
            cp.start()
            copies.append(cp)
        return copies

    def span(c):
        return BOUNDS[c], BOUNDS[c + 1] - BOUNDS[c]

    def project_slot(slot, lo, n):
        for value in range(2):
            @pl.when(slot == 1 + value)
            def _():
                project((1 + value,), lo, n, True)

    own_copy.wait()
    w_copies[0].wait()
    project_slot(own, 0, HALF)
    for c in range(2):
        part[c].wait_recv()
        relay[c].start()
        project_slot(other, *span(c))
    w_copies[1].wait()
    scattered = []
    for c in range(CHUNKS):
        outer[c].wait_recv()
        relay[c].wait_recv()
        project((0, 3), *span(c), False)
        temporal(c)
        scattered.append(scatter(c))
        if c == 0:
            part[2].wait_recv()
            relay[2].start()
            project_slot(other, *span(2))
    left_copies = []
    pltpu.make_async_copy(lft.at[side], rcl.at[me], csem.at[3]).start()
    for k in range(1, 4):
        s, device = peer(k)
        cp = remote(lft.at[side], rcl.at[me], lsnd.at[k], lrcv.at[k], device)
        cp.start()
        left_copies.append(cp)
    w_copies[2].wait()
    w_copies[3].wait()

    def gather(c):
        last = c == CHUNKS - 1
        pltpu.make_async_copy(snd.at[c, gid], recv.at[c, gid], csem.at[c]).wait()
        for cp in scattered[c]:
            cp.wait_recv()
        rows = 320 if last else 256

        moved = dot(perm2[...], recv[c].reshape(256, WIDTH)).astype(BF16)
        xs[:, 64 * c:64 * c + 64] = moved.reshape(4, 64, WIDTH)
        nrm2[0:256] = norm_rows(moved, gain_s[...].reshape(1, WIDTH))
        if last:
            pltpu.make_async_copy(lft.at[side], rcl.at[me], csem.at[3]).wait()
            for cp in left_copies:
                cp.wait_recv()
            moved = dot(perm3[0], rcl[...].reshape(64, WIDTH)).astype(BF16)
            xs[:, 192:208] = moved.reshape(4, 16, WIDTH)
            nrm2[256:320] = norm_rows(moved, gain_s[...].reshape(1, WIDTH))
        for j in range(3):
            cols = slice(WIDTH * j, WIDTH * j + WIDTH)
            tile = dot(nrm2[0:rows], wsq[:, cols]).astype(BF16)
            if j == 0:
                tile = tile * jnp.asarray(0.125, BF16)
            qkv[:, 64 * c:64 * c + 64, cols] = tile[0:256].reshape(4, 64, WIDTH)
            if last:
                qkv[:, 192:208, cols] = tile[256:320].reshape(4, 16, WIDTH)

    for c in range(CHUNKS):
        gather(c)

    lane128 = lax.broadcasted_iota(jnp.int32, (1, 128), 1)
    low = lane128 < 64
    low_b = jnp.where(low, 1.0, 0.0).astype(BF16)
    high_b = jnp.where(low, 0.0, 1.0).astype(BF16)
    key_ok = lax.broadcasted_iota(jnp.int32, (1, TOKENS), 1) < VALID

    def frame(f, _):
        for j in range(HEADS // 2):
            cols = slice(128 * j, 128 * j + 128)
            query = qkv[f, :, cols]
            keys = qkv[f, :, WIDTH + 128 * j:WIDTH + 128 * j + 128]
            vals = qkv[f, :, 2 * WIDTH + 128 * j:2 * WIDTH + 128 * j + 128]
            parts = []
            for mine, rest in ((low_b, high_b), (high_b, low_b)):
                score = lax.dot_general(query * mine, keys, NT, preferred_element_type=F32)
                score = jnp.where(key_ok, score, NINF)
                raised = jnp.exp(score - jnp.max(score, axis=-1, keepdims=True)).astype(BF16)
                parts.append(dot(raised, vals * mine + rest))
            top = jnp.where(low, parts[0], parts[1])
            total = pltpu.roll(jnp.where(low, parts[1], parts[0]), 64, 1)
            smix[:, cols] = (top / total).astype(BF16)
        done = (xs[f].astype(F32) + dot(smix[...], wso[...])).astype(BF16)
        om[f] = done[0:192].reshape(3, 4, 16, WIDTH)
        ol[f] = done[192:208]
        pltpu.make_async_copy(om.at[f, :, me], ret.at[4 * me + f], tsnd.at[f, 0]).start()
        for k in range(1, 4):
            s, device = peer(k)
            remote(om.at[f, :, s], ret.at[4 * me + f], tsnd.at[f, k], trcv.at[f, k], device).start()
        return 0

    lax.fori_loop(0, 4, frame, 0)

    rl[...] = dot(perm3[1], ol[...].reshape(64, WIDTH)).astype(BF16).reshape(4, 16, WIDTH)
    pltpu.make_async_copy(rl.at[me], retl.at[me], usnd.at[0]).start()
    for k in range(1, 4):
        s, device = peer(k)
        remote(rl.at[s], retl.at[me], usnd.at[k], urcv.at[k], device).start()

    for f in range(4):
        pltpu.make_async_copy(om.at[f, :, me], ret.at[4 * me + f], tsnd.at[f, 0]).wait()
        for k in range(1, 4):
            s, device = peer(k)
            remote(om.at[f, :, s], ret.at[4 * me + f], tsnd.at[f, k], trcv.at[f, k], device).wait()

    for c in range(CHUNKS):
        moved = dot(perm5[...], ret[:, c].reshape(256, WIDTH)).astype(BF16).reshape(16, 16, WIDTH)
        out[8 * c:8 * c + 8] = moved[0:8]
        out[25 + 8 * c:33 + 8 * c] = moved[8:16]
    pltpu.make_async_copy(rl.at[me], retl.at[me], usnd.at[0]).wait()
    for k in range(1, 4):
        s, device = peer(k)
        remote(rl.at[s], retl.at[me], usnd.at[k], urcv.at[k], device).wait()
    out[24] = (retl[0] + retl[1]) + (retl[2] + retl[3])

    for c in range(CHUNKS):
        part[c].wait_send()
        outer[c].wait_send()
        relay[c].wait_send()
        for cp in scattered[c]:
            cp.wait_send()
    for cp in left_copies:
        cp.wait_send()


def on_device(frames_in, ln_time, w_time_qkv, w_time_out, ln_space, w_space_qkv, w_space_out, band_lo, band_hi, valid):
    x = jnp.transpose(frames_in, (1, 0, 2))
    any_spec = pl.BlockSpec(memory_space=pl.ANY)
    vmem_spec = pl.BlockSpec(memory_space=pltpu.VMEM)
    smem_spec = pl.BlockSpec(memory_space=pltpu.SMEM)
    dma = pltpu.SemaphoreType.DMA
    scratch = [
        pltpu.VMEM((WIDTH, 3 * WIDTH), BF16),
        pltpu.VMEM((WIDTH, WIDTH), BF16),
        pltpu.VMEM((WIDTH, 3 * WIDTH), BF16),
        pltpu.VMEM((WIDTH, WIDTH), BF16),
        pltpu.VMEM((4, HALF, BLOCK, WIDTH), BF16),
        pltpu.VMEM((400, WIDTH), BF16),
        pltpu.VMEM((4, 400, 2 * WIDTH), BF16),
        pltpu.VMEM((2, 400, WIDTH), BF16),
        pltpu.VMEM((288, WIDTH), BF16),
        pltpu.VMEM((CHUNKS, 8, 32, WIDTH), BF16),
        pltpu.VMEM((2, BLOCK, WIDTH), BF16),
        pltpu.VMEM((CHUNKS, 8, 32, WIDTH), BF16),
        pltpu.VMEM((4, BLOCK, WIDTH), BF16),
        pltpu.VMEM((4, TOKENS, WIDTH), BF16),
        pltpu.VMEM((320, WIDTH), BF16),
        pltpu.VMEM((4, TOKENS, 3 * WIDTH), BF16),
        pltpu.VMEM((TOKENS, WIDTH), BF16),
        pltpu.VMEM((4, CHUNKS, 4, BLOCK, WIDTH), BF16),
        pltpu.VMEM((4, BLOCK, WIDTH), BF16),
        pltpu.VMEM((BLOCK, CHUNKS, BLOCK, WIDTH), BF16),
        pltpu.VMEM((4, BLOCK, WIDTH), BF16),
        pltpu.VMEM((4, BLOCK, WIDTH), BF16),
        pltpu.VMEM((2, 8, 128), F32),
        pltpu.VMEM((128, 64), F32),
        pltpu.VMEM((128, 128), BF16),
        pltpu.VMEM((256, 256), BF16),
        pltpu.VMEM((2, 64, 64), BF16),
        pltpu.VMEM((256, 256), BF16),
        dma((5,)), dma((4,)),
        dma((3,)), dma((3,)), dma((3,)), dma((3,)), dma((3,)), dma((3,)), dma((2,)),
        dma((3, 8)), dma((3, 8)), dma((4,)), dma((4,)),
        dma((4, 4)), dma((4, 4)), dma((4,)), dma((4,)),
    ]
    result = pl.pallas_call(
        kernel,
        out_shape=jax.ShapeDtypeStruct((PATCH, BLOCK, WIDTH), BF16),
        in_specs=[any_spec] * 5 + [vmem_spec] * 2 + [smem_spec] * 3,
        out_specs=vmem_spec,
        scratch_shapes=scratch,
        compiler_params=pltpu.CompilerParams(
            collective_id=0, has_side_effects=True, vmem_limit_bytes=56 * 1024 * 1024
        ),
    )(
        x, w_time_qkv, w_time_out, w_space_qkv, w_space_out,
        ln_time, ln_space, band_lo, band_hi, valid,
    )
    return jnp.transpose(result, (1, 0, 2))


def solution(mesh):
    placed = (P("tm", "patch", None), P(), P(), P(), P(), P(), P(), P("tm"), P("tm"), P())
    return jax.shard_map(
        on_device, mesh=mesh, in_specs=placed, out_specs=P("tm", "patch", None), check_vma=False
    )
```

```python
import functools

import jax
import jax.numpy as jnp
from jax import lax
from jax.experimental import pallas as pl
from jax.experimental.pallas import tpu as pltpu
from jax.sharding import PartitionSpec as P

MESH = pl.DeviceIdType.MESH
F32 = jnp.float32
BF16 = jnp.bfloat16
HEADS = 12
BLOCK = 16
WIDTH = 768
PATCH = 49
HALF = 25
GROUP = 8
CHUNKS = 3
UNIT = 4
PIECES = 6
UNITS = ((0, 1), (2, 3), (4,), (5,))
BOUNDS = (0, 5, 9, 13, 17, 21, 25)
TOKENS = 208
VALID = 196
NT = (((1,), (1,)), ((), ()))
NINF = float("-inf")


def dot(a, b):
    return jnp.dot(a, b, preferred_element_type=F32)


def norm_rows(values, gain):
    floats = values.astype(F32)
    center = floats - jnp.mean(floats, axis=-1, keepdims=True)
    spread = jnp.mean(center * center, axis=-1, keepdims=True)
    return (center * lax.rsqrt(spread + 1e-05) * gain).astype(BF16)


def select_matrix(rows, cols, source):
    row = lax.broadcasted_iota(jnp.int32, (rows, cols), 0)
    col = lax.broadcasted_iota(jnp.int32, (rows, cols), 1)
    return jnp.where(source(row) == col, 1.0, 0.0).astype(BF16)


def bits(value, low, count):
    return (value >> low) & ((1 << count) - 1)


def kernel(
    x_hbm, wtq_hbm, wto_hbm, wsq_hbm, wso_hbm, gain_t, gain_s, band_lo, band_hi, valid, out,
    wtq, wto, wsq, wso, x4, nrm, kv, qs, mix, snd, lft, recv, rcl, xs, nrm2, qkv, smix,
    om, ol, ret, rl, retl, biasb, bias, perm1, perm2, perm3, perm4, perm5,
    lsem, csem, psnd, prcv, osnd, orcv, rsnd, rrcv, bsem,
    ssnd, srcv, lsnd, lrcv, tsnd, trcv, usnd, urcv,
):
    tm = lax.axis_index("tm")
    me = lax.axis_index("patch")
    pairs = lax.axis_size("tm") // 2
    pair = tm // 2
    side = tm % 2
    own = 1 + side
    other = 2 - side
    gid = side * 4 + me
    out_pair = (pair + 2 * side - 1 + pairs) % pairs
    rly_pair = (pair + 1 - 2 * side + pairs) % pairs
    partner = (pair * 2 + 1 - side, me)
    out_dev = (out_pair * 2 + side, me)
    rly_dev = (rly_pair * 2 + side, me)

    def member(k):
        d = (gid + k) % 8
        return d, (pair * 2 + d // 4, d % 4)

    def peer(k):
        s = (me + k) % 4
        return s, (tm, s)

    def remote(src, dst, snd_sem, rcv_sem, device):
        return pltpu.make_async_remote_copy(
            src_ref=src, dst_ref=dst, send_sem=snd_sem, recv_sem=rcv_sem,
            device_id=device, device_id_type=MESH,
        )

    own_copy = pltpu.make_async_copy(x_hbm.at[pl.ds(24 * side, HALF)], x4.at[own], lsem.at[0])
    own_copy.start()
    w_copies = []
    for i, (src, dst) in enumerate(((wtq_hbm, wtq), (wto_hbm, wto), (wsq_hbm, wsq), (wso_hbm, wso))):
        cp = pltpu.make_async_copy(src, dst, lsem.at[1 + i])
        cp.start()
        w_copies.append(cp)

    left_ok = (band_lo[0] <= -1) & (tm >= 1) & (valid[jnp.maximum(tm - 1, 0)] == 1)
    right_ok = (band_hi[0] >= 1) & (tm <= 2 * pairs - 2) & (valid[jnp.minimum(tm + 1, 2 * pairs - 1)] == 1)
    left = jnp.where(left_ok, 0.0, NINF)
    right = jnp.where(right_ok, 0.0, NINF)
    row8 = lax.broadcasted_iota(jnp.int32, (8, 128), 0)
    biasb[side] = jnp.where(row8 == 0, left, right)

    barrier = pltpu.get_barrier_semaphore()
    for k in range(1, 8):
        pl.semaphore_signal(barrier, inc=1, device_id=member(k)[1], device_id_type=MESH)
    pl.semaphore_signal(barrier, inc=1, device_id=out_dev, device_id_type=MESH)
    pl.semaphore_signal(barrier, inc=1, device_id=rly_dev, device_id_type=MESH)
    pl.semaphore_wait(barrier, 9)

    part, outer = [], []
    for c in range(PIECES):
        lo, n = BOUNDS[c], BOUNDS[c + 1] - BOUNDS[c]
        part.append(remote(
            x_hbm.at[pl.ds(24 * (1 - side) + lo, n)], x4.at[own, pl.ds(lo, n)],
            psnd.at[c], prcv.at[c], partner,
        ))
        outer.append(remote(
            x_hbm.at[pl.ds(24 * side + lo, n)], x4.at[3 - 3 * side, pl.ds(lo, n)],
            osnd.at[c], orcv.at[c], out_dev,
        ))
    relay = []
    for c in range(PIECES):
        lo, n = BOUNDS[c], BOUNDS[c + 1] - BOUNDS[c]
        relay.append(remote(
            x4.at[other, pl.ds(lo, n)], x4.at[3 * side, pl.ds(lo, n)],
            rsnd.at[c], rrcv.at[c], rly_dev,
        ))
    bias_copy = remote(biasb.at[side], biasb.at[side], bsem.at[0], bsem.at[1], partner)
    bias_copy.start()
    for c in range(PIECES):
        part[c].start()
        outer[c].start()

    perm1[...] = select_matrix(
        128, 128,
        lambda r: (bits(r, 6, 1) << 6) | (bits(r, 2, 2) << 4) | (bits(r, 4, 2) << 2) | bits(r, 0, 2),
    )
    perm4[...] = select_matrix(
        128, 128, lambda r: (bits(r, 2, 1) << 6) | (bits(r, 3, 2) << 4) | (bits(r, 0, 2) << 2) | bits(r, 5, 2)
    )
    perm2[...] = select_matrix(
        256, 256,
        lambda r: (bits(r, 3, 1) << 7) | (bits(r, 4, 2) << 5) | (bits(r, 0, 3) << 2) | bits(r, 6, 2),
    )
    perm5[...] = select_matrix(256, 256, lambda r: (bits(r, 0, 4) << 4) | bits(r, 4, 4))
    perm3[0] = select_matrix(
        64, 64, lambda r: jnp.where(bits(r, 0, 4) < 4, (bits(r, 0, 2) << 4) + me * 4 + bits(r, 4, 2), -1)
    )
    perm3[1] = select_matrix(
        64, 64, lambda r: jnp.where(bits(r, 2, 2) == me, (bits(r, 0, 2) << 4) + bits(r, 4, 2), -1)
    )

    lane256 = lax.broadcasted_iota(jnp.int32, (1, 256), 1) >> 6
    head_f = [lane256 == h for h in range(4)]
    head_b = [jnp.where(m, 1.0, 0.0).astype(BF16) for m in head_f]

    def project(slots, lo, n, queries):
        rows = 16 * n
        for i, slot in enumerate(slots):
            block = x4[slot, lo:lo + n].reshape(rows, WIDTH)
            nrm[rows * i:rows * i + rows] = norm_rows(block, gain_t[...].reshape(1, WIDTH))
        normed = nrm[0:rows * len(slots)]
        pairs_kv = dot(normed, wtq[:, WIDTH:]).astype(BF16)
        for i, slot in enumerate(slots):
            kv[slot, 16 * lo:16 * lo + rows] = pairs_kv[rows * i:rows * i + rows]
        if queries:
            query = dot(normed, wtq[:, 0:WIDTH]).astype(BF16) * jnp.asarray(0.125, BF16)
            qs[slots[0] - 1, 16 * lo:16 * lo + rows] = query

    def attend(places):
        scores, values = [], []
        for at, _ in places:
            q_all = [qs[b, pl.ds(at, 16)] for b in range(2)]
            for g in range(3):
                cols = slice(256 * g, 256 * g + 256)
                vcols = slice(768 + 256 * g, 768 + 256 * g + 256)
                keys = jnp.concatenate([kv[slot, pl.ds(at, 16), cols] for slot in range(4)], axis=0)
                values.append(jnp.concatenate([kv[slot, pl.ds(at, 16), vcols] for slot in range(4)], axis=0))
                query = jnp.concatenate([q[:, cols] for q in q_all], axis=0)
                stacked = jnp.concatenate([query * m for m in head_b], axis=0)
                scores.append(lax.dot_general(stacked, keys, NT, preferred_element_type=F32) + bias[...])
        tops = [jnp.max(score, axis=-1, keepdims=True) for score in scores]
        raised = [jnp.exp(score - top) for score, top in zip(scores, tops)]
        scales = [1.0 / jnp.sum(r, axis=-1, keepdims=True) for r in raised]
        weights = [(r * scale).astype(BF16) for r, scale in zip(raised, scales)]
        mixed = [dot(weight, value) for weight, value in zip(weights, values)]
        for i, part_mix in enumerate(mixed):
            rows, cols = places[i // 3][1], slice(256 * (i % 3), 256 * (i % 3) + 256)
            picked = jnp.where(head_f[0], part_mix[0:32], 0.0)
            for h in range(1, 4):
                picked = jnp.where(head_f[h], part_mix[32 * h:32 * h + 32], picked)
            picked = picked.astype(BF16)
            mix[rows[0]:rows[0] + 16, cols] = picked[:16]
            mix[rows[1]:rows[1] + 16, cols] = picked[16:]

    lo_at = 24 - 24 * side

    def temporal(u):
        subs, last = UNITS[u], u == len(UNITS) - 1
        rows = 128 * len(subs)
        places = []
        for i, sub in enumerate(subs):
            for j in range(UNIT):
                at = pl.multiple_of((side + UNIT * sub + j) * 16, 16)
                places.append((at, (128 * i + 16 * j, 128 * i + 64 + 16 * j)))
        if last:
            places.append((pl.multiple_of(lo_at * 16, 16), (rows, rows + 16)))
        attend(places)
        acc = dot(mix[0:rows + 32 if last else rows], wto[...])
        for i, sub in enumerate(subs):
            base = x4[1:3, pl.ds(side + UNIT * sub, UNIT)].reshape(128, WIDTH)
            after = (base.astype(F32) + acc[128 * i:128 * i + 128]).astype(BF16)
            moved = dot(perm1[...], after).astype(BF16)
            half = 16 * (sub % 2)
            snd[sub // 2, :, half:half + 16] = moved.reshape(8, 16, WIDTH)
        if last:
            base = x4[1:3, lo_at].reshape(32, WIDTH)
            lft[...] = (base.astype(F32) + acc[rows:rows + 32]).astype(BF16).reshape(2, 16, WIDTH)

    def lines(u):
        return UNITS[u][0] // 2, pl.ds(16 * (UNITS[u][0] % 2), 16 * len(UNITS[u]))

    def own_piece(u):
        c, rows = lines(u)
        return pltpu.make_async_copy(snd.at[c, gid, rows], recv.at[c, gid, rows], csem.at[u])

    def scatter(u):
        c, rows = lines(u)
        copies = []
        own_piece(u).start()
        for k in (2, 6, 4, 3, 5, 1, 7):
            d, device = member(k)
            cp = remote(snd.at[c, d, rows], recv.at[c, gid, rows], ssnd.at[u, k], srcv.at[u, k], device)
            cp.start()
            copies.append(cp)
        return copies

    def span(first, count):
        return BOUNDS[first], BOUNDS[first + count] - BOUNDS[first]

    def project_slot(slot, lo, n):
        for value in range(2):
            @pl.when(slot == 1 + value)
            def _():
                project((1 + value,), lo, n, True)

    own_copy.wait()
    w_copies[0].wait()
    project_slot(own, 0, HALF)

    bias_copy.wait()
    key_slot = lax.broadcasted_iota(jnp.int32, (32, 64), 1) >> 4
    query_blk = lax.broadcasted_iota(jnp.int32, (32, 64), 0) >> 4
    offset = key_slot - 1 - query_blk
    one = jnp.where(
        query_blk == 0,
        jnp.where(offset < 0, biasb[0, 0:1, 0:64], biasb[0, 1:2, 0:64]),
        jnp.where(offset < 0, biasb[1, 0:1, 0:64], biasb[1, 1:2, 0:64]),
    )
    one = jnp.where(offset == 0, 0.0, one)
    one = jnp.where((offset > 1) | (offset < -1), NINF, one)
    for h in range(4):
        bias[32 * h:32 * h + 32] = one

    w_copies[1].wait()
    scattered = []

    def forward(*pieces):
        for c in pieces:
            part[c].wait_recv()
            relay[c].start()

    def halos(*pieces):
        for c in pieces:
            outer[c].wait_recv()
            relay[c].wait_recv()
        project((0, 3), *span(pieces[0], len(pieces)), False)

    def unit(u):
        temporal(u)
        scattered.append(scatter(u))

    forward(0, 1)
    project_slot(other, *span(0, 2))
    forward(2)
    halos(0, 1)
    forward(3)
    project_slot(other, *span(2, 2))
    unit(0)
    forward(4)
    halos(2, 3)
    forward(5)
    project_slot(other, *span(4, 2))
    unit(1)
    halos(4)
    unit(2)
    halos(5)
    unit(3)
    left_copies = []
    pltpu.make_async_copy(lft.at[side], rcl.at[me], csem.at[len(UNITS)]).start()
    for k in range(1, 4):
        s, device = peer(k)
        cp = remote(lft.at[side], rcl.at[me], lsnd.at[k], lrcv.at[k], device)
        cp.start()
        left_copies.append(cp)
    w_copies[2].wait()
    w_copies[3].wait()

    def gather(u):
        last = u == len(UNITS) - 1
        c, lines_u = lines(u)
        rows = 128 * len(UNITS[u])
        count = rows // 4
        at = 64 * c + 32 * (UNITS[u][0] % 2)
        own_piece(u).wait()
        for cp in scattered[u]:
            cp.wait_recv()
        perm = perm2 if rows == 256 else perm4
        moved = dot(perm[...], recv[c, :, lines_u].reshape(rows, WIDTH)).astype(BF16)
        xs[:, at:at + count] = moved.reshape(4, count, WIDTH)
        nrm2[0:rows] = norm_rows(moved, gain_s[...].reshape(1, WIDTH))
        total = rows
        if last:
            pltpu.make_async_copy(lft.at[side], rcl.at[me], csem.at[len(UNITS)]).wait()
            for cp in left_copies:
                cp.wait_recv()
            moved = dot(perm3[0], rcl[...].reshape(64, WIDTH)).astype(BF16)
            xs[:, 192:208] = moved.reshape(4, 16, WIDTH)
            nrm2[rows:rows + 64] = norm_rows(moved, gain_s[...].reshape(1, WIDTH))
            total = rows + 64
        for j in range(3):
            cols = slice(WIDTH * j, WIDTH * j + WIDTH)
            tile = dot(nrm2[0:total], wsq[:, cols]).astype(BF16)
            if j == 0:
                tile = tile * jnp.asarray(0.125, BF16)
            qkv[:, at:at + count, cols] = tile[0:rows].reshape(4, count, WIDTH)
            if last:
                qkv[:, 192:208, cols] = tile[rows:total].reshape(4, 16, WIDTH)

    for u in range(len(UNITS)):
        gather(u)

    lane128 = lax.broadcasted_iota(jnp.int32, (1, 128), 1)
    low = lane128 < 64
    low_b = jnp.where(low, 1.0, 0.0).astype(BF16)
    high_b = jnp.where(low, 0.0, 1.0).astype(BF16)
    key_ok = lax.broadcasted_iota(jnp.int32, (1, TOKENS), 1) < VALID

    def frame(f, _):
        for first in (0, 3):
            group = range(first, first + 3)
            scores, values = [], []
            for j in group:
                query = qkv[f, :, 128 * j:128 * j + 128]
                keys = qkv[f, :, WIDTH + 128 * j:WIDTH + 128 * j + 128]
                vals = qkv[f, :, 2 * WIDTH + 128 * j:2 * WIDTH + 128 * j + 128]
                for mine, rest in ((low_b, high_b), (high_b, low_b)):
                    score = lax.dot_general(query * mine, keys, NT, preferred_element_type=F32)
                    scores.append(jnp.where(key_ok, score, NINF))
                    values.append(vals * mine + rest)
            tops = [jnp.max(score, axis=-1, keepdims=True) for score in scores]
            raised = [jnp.exp(score - top).astype(BF16) for score, top in zip(scores, tops)]
            parts = [dot(r, value) for r, value in zip(raised, values)]
            for i, j in enumerate(group):
                even, odd = parts[2 * i], parts[2 * i + 1]
                total = pltpu.roll(jnp.where(low, odd, even), 64, 1)
                smix[:, 128 * j:128 * j + 128] = (jnp.where(low, even, odd) / total).astype(BF16)
        done = xs[f].astype(F32) + dot(smix[...], wso[...])
        om[f, 0:2] = done[0:128].astype(BF16).reshape(2, 4, 16, WIDTH)
        halves = [done[128 + 32 * i:160 + 32 * i].reshape(4, 8, WIDTH) for i in range(2)]
        om[f, 2] = jnp.concatenate(halves, axis=1).astype(BF16)
        ol[f] = done[192:208].astype(BF16)
        pltpu.make_async_copy(om.at[f, :, me], ret.at[4 * me + f], tsnd.at[f, 0]).start()
        for k in (2, 1, 3):
            s, device = peer(k)
            remote(om.at[f, :, s], ret.at[4 * me + f], tsnd.at[f, k], trcv.at[f, k], device).start()
        return 0

    lax.fori_loop(0, 4, frame, 0)

    rl[...] = dot(perm3[1], ol[...].reshape(64, WIDTH)).astype(BF16).reshape(4, 16, WIDTH)
    pltpu.make_async_copy(rl.at[me], retl.at[me], usnd.at[0]).start()
    for k in range(1, 4):
        s, device = peer(k)
        remote(rl.at[s], retl.at[me], usnd.at[k], urcv.at[k], device).start()

    for f in range(4):
        pltpu.make_async_copy(om.at[f, :, me], ret.at[4 * me + f], tsnd.at[f, 0]).wait()
        for k in (2, 1, 3):
            s, device = peer(k)
            remote(om.at[f, :, s], ret.at[4 * me + f], tsnd.at[f, k], trcv.at[f, k], device).wait()

    for c in range(CHUNKS):
        moved = dot(perm5[...], ret[:, c].reshape(256, WIDTH)).astype(BF16).reshape(16, 16, WIDTH)
        for i in range(2):
            low_at, high_at = (8 * i, 8 * i + 4) if c == 2 else (4 * i, 4 * i + 8)
            out[8 * c + 4 * i:8 * c + 4 * i + 4] = moved[low_at:low_at + 4]
            out[25 + 8 * c + 4 * i:29 + 8 * c + 4 * i] = moved[high_at:high_at + 4]
    pltpu.make_async_copy(rl.at[me], retl.at[me], usnd.at[0]).wait()
    for k in range(1, 4):
        s, device = peer(k)
        remote(rl.at[s], retl.at[me], usnd.at[k], urcv.at[k], device).wait()
    out[24] = (retl[0] + retl[1]) + (retl[2] + retl[3])

    for c in range(PIECES):
        part[c].wait_send()
        outer[c].wait_send()
        relay[c].wait_send()
    for copies in scattered:
        for cp in copies:
            cp.wait_send()
    for cp in left_copies:
        cp.wait_send()


def on_device(frames_in, ln_time, w_time_qkv, w_time_out, ln_space, w_space_qkv, w_space_out, band_lo, band_hi, valid):
    x = jnp.transpose(frames_in, (1, 0, 2))
    any_spec = pl.BlockSpec(memory_space=pl.ANY)
    vmem_spec = pl.BlockSpec(memory_space=pltpu.VMEM)
    smem_spec = pl.BlockSpec(memory_space=pltpu.SMEM)
    dma = pltpu.SemaphoreType.DMA
    scratch = [
        pltpu.VMEM((WIDTH, 3 * WIDTH), BF16),
        pltpu.VMEM((WIDTH, WIDTH), BF16),
        pltpu.VMEM((WIDTH, 3 * WIDTH), BF16),
        pltpu.VMEM((WIDTH, WIDTH), BF16),
        pltpu.VMEM((4, HALF, BLOCK, WIDTH), BF16),
        pltpu.VMEM((400, WIDTH), BF16),
        pltpu.VMEM((4, 400, 2 * WIDTH), BF16),
        pltpu.VMEM((2, 400, WIDTH), BF16),
        pltpu.VMEM((256, WIDTH), BF16),
        pltpu.VMEM((CHUNKS, 8, 32, WIDTH), BF16),
        pltpu.VMEM((2, BLOCK, WIDTH), BF16),
        pltpu.VMEM((CHUNKS, 8, 32, WIDTH), BF16),
        pltpu.VMEM((4, BLOCK, WIDTH), BF16),
        pltpu.VMEM((4, TOKENS, WIDTH), BF16),
        pltpu.VMEM((320, WIDTH), BF16),
        pltpu.VMEM((4, TOKENS, 3 * WIDTH), BF16),
        pltpu.VMEM((TOKENS, WIDTH), BF16),
        pltpu.VMEM((4, CHUNKS, 4, BLOCK, WIDTH), BF16),
        pltpu.VMEM((4, BLOCK, WIDTH), BF16),
        pltpu.VMEM((BLOCK, CHUNKS, BLOCK, WIDTH), BF16),
        pltpu.VMEM((4, BLOCK, WIDTH), BF16),
        pltpu.VMEM((4, BLOCK, WIDTH), BF16),
        pltpu.VMEM((2, 8, 128), F32),
        pltpu.VMEM((128, 64), F32),
        pltpu.VMEM((128, 128), BF16),
        pltpu.VMEM((256, 256), BF16),
        pltpu.VMEM((2, 64, 64), BF16),
        pltpu.VMEM((128, 128), BF16),
        pltpu.VMEM((256, 256), BF16),
        dma((5,)), dma((len(UNITS) + 1,)),
        *[dma((PIECES,))] * 6, dma((2,)),
        dma((len(UNITS), 8)), dma((len(UNITS), 8)), dma((4,)), dma((4,)),
        dma((4, 4)), dma((4, 4)), dma((4,)), dma((4,)),
    ]
    result = pl.pallas_call(
        kernel,
        out_shape=pltpu.VMEM((PATCH, BLOCK, WIDTH), BF16),
        in_specs=[any_spec] * 5 + [vmem_spec] * 2 + [smem_spec] * 3,
        out_specs=vmem_spec,
        scratch_shapes=scratch,
        compiler_params=pltpu.CompilerParams(
            collective_id=0, has_side_effects=True, vmem_limit_bytes=56 * 1024 * 1024
        ),
    )(
        x, w_time_qkv, w_time_out, w_space_qkv, w_space_out,
        ln_time, ln_space, band_lo, band_hi, valid,
    )
    return jnp.transpose(result, (1, 0, 2))


def solution(mesh):
    placed = (P("tm", "patch", None), P(), P(), P(), P(), P(), P(), P("tm"), P("tm"), P())
    return jax.shard_map(
        on_device, mesh=mesh, in_specs=placed, out_specs=P("tm", "patch", None), check_vma=False
    )
```

```python
import functools

import jax
import jax.numpy as jnp
from jax import lax
from jax.experimental import pallas as pl
from jax.experimental.pallas import tpu as pltpu
from jax.sharding import PartitionSpec as P

MESH = pl.DeviceIdType.MESH
F32 = jnp.float32
BF16 = jnp.bfloat16
HEADS = 12
BLOCK = 16
WIDTH = 768
PATCH = 49
HALF = 25
GROUP = 8
CHUNKS = 3
PIECES = 9
PARCELS = ((0, 0), (0, 16), (1, 0), (1, 16), (2, 0), (2, 16))
BOUNDS = (0, 1, 3, 6, 9, 13, 17, 21, 23, 25)
TOKENS = 208
VALID = 196
NT = (((1,), (1,)), ((), ()))
NINF = float("-inf")


def dot(a, b):
    return jnp.dot(a, b, preferred_element_type=F32)


def norm_rows(values, gain):
    floats = values.astype(F32)
    center = floats - jnp.mean(floats, axis=-1, keepdims=True)
    spread = jnp.mean(center * center, axis=-1, keepdims=True)
    return (center * lax.rsqrt(spread + 1e-05) * gain).astype(BF16)


def select_matrix(rows, cols, source):
    row = lax.broadcasted_iota(jnp.int32, (rows, cols), 0)
    col = lax.broadcasted_iota(jnp.int32, (rows, cols), 1)
    return jnp.where(source(row) == col, 1.0, 0.0).astype(BF16)


def bits(value, low, count):
    return (value >> low) & ((1 << count) - 1)


def kernel(
    x_hbm, wtq_hbm, wto_hbm, wsq_hbm, wso_hbm, gain_t, gain_s, band_lo, band_hi, valid, out,
    wtq, wto, wsq, wso, x4, nrm, kv, qs, mix, snd, lft, recv, rcl, xs, nrm2, qkv, smix,
    om, ol, ret, rl, retl, biasb, bias, perm3, perm6, perm7, perm5,
    lsem, csem, psnd, prcv, rsnd, rrcv, bsem,
    ssnd, srcv, lsnd, lrcv, tsnd, trcv, usnd, urcv,
):
    tm = lax.axis_index("tm")
    me = lax.axis_index("patch")
    pairs = lax.axis_size("tm") // 2
    pair = tm // 2
    side = tm % 2
    own = 1 + side
    gid = side * 4 + me
    home = (me + 2) % 4
    slot_id = side * 4 + home
    partner = (pair * 2 + 1 - side, me)
    before = ((pair - 1 + pairs) % pairs * 2 + side, me)
    behind = ((pair + 1) % pairs * 2 + side, me)

    def member(k):
        d = (gid + k) % 8
        return d, (pair * 2 + d // 4, d % 4)

    def peer(k):
        s = (me + k) % 4
        return s, (tm, s)

    def remote(src, dst, snd_sem, rcv_sem, device):
        return pltpu.make_async_remote_copy(
            src_ref=src, dst_ref=dst, send_sem=snd_sem, recv_sem=rcv_sem,
            device_id=device, device_id_type=MESH,
        )

    w_copies = []
    for i, (src, dst) in enumerate(((wtq_hbm, wtq), (wto_hbm, wto), (wsq_hbm, wsq), (wso_hbm, wso))):
        cp = pltpu.make_async_copy(src, dst, lsem.at[1 + i])
        cp.start()
        w_copies.append(cp)

    left_ok = (band_lo[0] <= -1) & (tm >= 1) & (valid[jnp.maximum(tm - 1, 0)] == 1)
    right_ok = (band_hi[0] >= 1) & (tm <= 2 * pairs - 2) & (valid[jnp.minimum(tm + 1, 2 * pairs - 1)] == 1)
    left = jnp.where(left_ok, 0.0, NINF)
    right = jnp.where(right_ok, 0.0, NINF)
    row8 = lax.broadcasted_iota(jnp.int32, (8, 128), 0)
    biasb[side] = jnp.where(row8 == 0, left, right)

    barrier = pltpu.get_barrier_semaphore()
    for k in range(1, 8):
        pl.semaphore_signal(barrier, inc=1, device_id=member(k)[1], device_id_type=MESH)
    pl.semaphore_signal(barrier, inc=1, device_id=before, device_id_type=MESH)
    pl.semaphore_signal(barrier, inc=1, device_id=behind, device_id_type=MESH)
    pl.semaphore_wait(barrier, 9)

    def piece(c):
        return pl.ds(BOUNDS[c], BOUNDS[c + 1] - BOUNDS[c])

    part, relay = [], []
    for c in range(PIECES):
        lo, n = BOUNDS[c], BOUNDS[c + 1] - BOUNDS[c]
        part.append([
            remote(
                x_hbm.at[pl.ds(25 * half + lo - 1 if c else 24, n)], x4.at[own, piece(c)],
                psnd.at[half, c], prcv.at[side, c], (pair * 2 + half, home),
            )
            for half in range(2)
        ])
        relay.append([
            remote(x4.at[1, piece(c)], x4.at[3, piece(c)], rsnd.at[0, c], rrcv.at[0, c], before),
            remote(x4.at[2, piece(c)], x4.at[0, piece(c)], rsnd.at[1, c], rrcv.at[1, c], behind),
        ])
    bias_copy = remote(biasb.at[side], biasb.at[side], bsem.at[0], bsem.at[1], partner)
    bias_copy.start()
    for c in range(PIECES):
        for cp in part[c]:
            cp.start()

    perm6[...] = select_matrix(
        256, 256,
        lambda r: (bits(r, 7, 1) << 7) | (bits(r, 1, 3) << 4) | (bits(r, 5, 2) << 2)
        | (bits(r, 4, 1) << 1) | bits(r, 0, 1),
    )
    perm7[...] = select_matrix(
        128, 128, lambda r: (bits(r, 3, 1) << 6) | (bits(r, 4, 2) << 4) | (bits(r, 0, 3) << 1) | bits(r, 6, 1)
    )
    perm5[...] = select_matrix(256, 256, lambda r: (bits(r, 0, 4) << 4) | bits(r, 4, 4))
    perm3[0] = select_matrix(
        64, 64, lambda r: jnp.where(bits(r, 0, 4) < 4, (bits(r, 0, 2) << 4) + me * 4 + bits(r, 4, 2), -1)
    )
    perm3[1] = select_matrix(
        64, 64, lambda r: jnp.where(bits(r, 2, 2) == me, (bits(r, 0, 2) << 4) + bits(r, 4, 2), -1)
    )

    lane256 = lax.broadcasted_iota(jnp.int32, (1, 256), 1) >> 6
    head_f = [lane256 == h for h in range(4)]
    head_b = [jnp.where(m, 1.0, 0.0).astype(BF16) for m in head_f]

    def project(slots, lo, n, queries):
        rows = 16 * n
        for i, slot in enumerate(slots):
            block = x4[slot, lo:lo + n].reshape(rows, WIDTH)
            nrm[rows * i:rows * i + rows] = norm_rows(block, gain_t[...].reshape(1, WIDTH))
        normed = nrm[0:rows * len(slots)]
        pairs_kv = dot(normed, wtq[:, WIDTH:]).astype(BF16)
        for i, slot in enumerate(slots):
            kv[slot, 16 * lo:16 * lo + rows] = pairs_kv[rows * i:rows * i + rows]
        if queries:
            query = dot(normed, wtq[:, 0:WIDTH]).astype(BF16) * jnp.asarray(0.125, BF16)
            for i in range(2):
                qs[i, 16 * lo:16 * lo + rows] = query[rows * i:rows * i + rows]

    def attend(places):
        scores, values = [], []
        for at, _ in places:
            q_all = [qs[b, at:at + 16] for b in range(2)]
            for g in range(3):
                cols = slice(256 * g, 256 * g + 256)
                vcols = slice(768 + 256 * g, 768 + 256 * g + 256)
                keys = jnp.concatenate([kv[slot, at:at + 16, cols] for slot in range(4)], axis=0)
                values.append(jnp.concatenate([kv[slot, at:at + 16, vcols] for slot in range(4)], axis=0))
                query = jnp.concatenate([q[:, cols] for q in q_all], axis=0)
                stacked = jnp.concatenate([query * m for m in head_b], axis=0)
                scores.append(lax.dot_general(stacked, keys, NT, preferred_element_type=F32) + bias[...])
        tops = [jnp.max(score, axis=-1, keepdims=True) for score in scores]
        raised = [jnp.exp(score - top) for score, top in zip(scores, tops)]
        scales = [1.0 / jnp.sum(r, axis=-1, keepdims=True) for r in raised]
        weights = [(r * scale).astype(BF16) for r, scale in zip(raised, scales)]
        mixed = [dot(weight, value) for weight, value in zip(weights, values)]
        for i, part_mix in enumerate(mixed):
            rows, cols = places[i // 3][1], slice(256 * (i % 3), 256 * (i % 3) + 256)
            picked = jnp.where(head_f[0], part_mix[0:32], 0.0)
            for h in range(1, 4):
                picked = jnp.where(head_f[h], part_mix[32 * h:32 * h + 32], picked)
            picked = picked.astype(BF16)
            mix[rows[0]:rows[0] + 16, cols] = picked[:16]
            mix[rows[1]:rows[1] + 16, cols] = picked[16:]

    def mix_unit(u):
        places = [(16 * (1 + GROUP * u + j), (16 * j, 128 + 16 * j)) for j in range(GROUP)]
        attend(places + [(0, (256, 272))] if u == 0 else places)

    def send_unit(u):
        first = 1 + GROUP * u
        acc = dot(mix[0:288 if u == 0 else 256], wto[...])
        base = x4[1:3, first:first + GROUP].reshape(256, WIDTH)
        after = (base.astype(F32) + acc[0:256]).astype(BF16)
        snd[u] = dot(perm6[...], after).astype(BF16).reshape(8, 32, WIDTH)
        if u == 0:
            base = x4[1:3, 0].reshape(32, WIDTH)
            lft[...] = (base.astype(F32) + acc[256:288]).astype(BF16).reshape(2, 16, WIDTH)
        scatter(2 * u)

    def own_piece(p):
        c, at = PARCELS[p]
        rows = pl.ds(at, 16)
        return pltpu.make_async_copy(snd.at[c, gid, rows], recv.at[c, slot_id, rows], csem.at[p])

    scattered = {}

    def scatter(p):
        c, at = PARCELS[p]
        rows = pl.ds(at, 16)
        scattered[p] = []
        own_piece(p).start()
        for k in (2, 6, 4, 3, 5, 1, 7):
            d, device = member(k)
            cp = remote(snd.at[c, d, rows], recv.at[c, slot_id, rows], ssnd.at[p, k], srcv.at[p, k], device)
            cp.start()
            scattered[p].append(cp)

    def span(first, count):
        return BOUNDS[first], BOUNDS[first + count] - BOUNDS[first]

    bias_copy.wait()
    key_slot = lax.broadcasted_iota(jnp.int32, (32, 64), 1) >> 4
    query_blk = lax.broadcasted_iota(jnp.int32, (32, 64), 0) >> 4
    offset = key_slot - 1 - query_blk
    one = jnp.where(
        query_blk == 0,
        jnp.where(offset < 0, biasb[0, 0:1, 0:64], biasb[0, 1:2, 0:64]),
        jnp.where(offset < 0, biasb[1, 0:1, 0:64], biasb[1, 1:2, 0:64]),
    )
    one = jnp.where(offset == 0, 0.0, one)
    one = jnp.where((offset > 1) | (offset < -1), NINF, one)
    for h in range(4):
        bias[32 * h:32 * h + 32] = one

    w_copies[0].wait()
    w_copies[1].wait()

    def forward(c):
        for b in range(2):
            remote(
                x4.at[1 + b, piece(c)], x4.at[1 + b, piece(c)], psnd.at[b, c], prcv.at[b, c], partner
            ).wait_recv()
            relay[c][b].start()

    def mine(*pieces):
        project((1, 2), *span(pieces[0], len(pieces)), True)

    def halos(*pieces):
        for c in pieces:
            for cp in relay[c]:
                cp.wait_recv()

    def beside(*pieces):
        project((0, 3), *span(pieces[0], len(pieces)), False)

    for c in range(4):
        forward(c)
    mine(0, 1, 2, 3)
    forward(4)
    mine(4)
    halos(0, 1, 2, 3)
    forward(5)
    beside(0, 1, 2, 3)
    mix_unit(0)
    forward(6)
    send_unit(0)
    left_copies = []
    pltpu.make_async_copy(lft.at[side], rcl.at[home], csem.at[len(PARCELS)]).start()
    for k in range(1, 4):
        s, device = peer(k)
        cp = remote(lft.at[side], rcl.at[home], lsnd.at[k], lrcv.at[k], device)
        cp.start()
        left_copies.append(cp)
    forward(7)
    mine(5, 6)
    forward(8)
    halos(4, 5)
    beside(4, 5)
    mix_unit(1)
    send_unit(1)
    mine(7, 8)
    halos(6, 7, 8)
    beside(6, 7, 8)
    mix_unit(2)
    send_unit(2)
    for p in (1, 3, 5):
        scatter(p)
    w_copies[2].wait()
    w_copies[3].wait()

    def gather(p):
        c, first = PARCELS[p]
        last, at = p == 0, 64 * c
        frames = slice(first // 8, first // 8 + 2)
        own_piece(p).wait()
        for cp in scattered[p]:
            cp.wait_recv()
        moved = dot(perm7[...], recv[c, :, first:first + 16].reshape(128, WIDTH)).astype(BF16)
        xs[frames, at:at + 64] = moved.reshape(2, 64, WIDTH)
        nrm2[0:128] = norm_rows(moved, gain_s[...].reshape(1, WIDTH))
        total = 128
        if last:
            pltpu.make_async_copy(lft.at[side], rcl.at[home], csem.at[len(PARCELS)]).wait()
            for cp in left_copies:
                cp.wait_recv()
            moved = dot(perm3[0], rcl[...].reshape(64, WIDTH)).astype(BF16)
            xs[:, 192:208] = moved.reshape(4, 16, WIDTH)
            nrm2[128:192] = norm_rows(moved, gain_s[...].reshape(1, WIDTH))
            total = 192
        for j in range(3):
            cols = slice(WIDTH * j, WIDTH * j + WIDTH)
            tile = dot(nrm2[0:total], wsq[:, cols]).astype(BF16)
            if j == 0:
                tile = tile * jnp.asarray(0.125, BF16)
            qkv[frames, at:at + 64, cols] = tile[0:128].reshape(2, 64, WIDTH)
            if last:
                qkv[:, 192:208, cols] = tile[128:192].reshape(4, 16, WIDTH)

    lane128 = lax.broadcasted_iota(jnp.int32, (1, 128), 1)
    low = lane128 < 64
    low_b = jnp.where(low, 1.0, 0.0).astype(BF16)
    high_b = jnp.where(low, 0.0, 1.0).astype(BF16)
    key_ok = lax.broadcasted_iota(jnp.int32, (1, TOKENS), 1) < VALID

    def frame(f, _):
        for first in (0, 3):
            group = range(first, first + 3)
            scores, values = [], []
            for j in group:
                query = qkv[f, :, 128 * j:128 * j + 128]
                keys = qkv[f, :, WIDTH + 128 * j:WIDTH + 128 * j + 128]
                vals = qkv[f, :, 2 * WIDTH + 128 * j:2 * WIDTH + 128 * j + 128]
                for mine, rest in ((low_b, high_b), (high_b, low_b)):
                    score = lax.dot_general(query * mine, keys, NT, preferred_element_type=F32)
                    scores.append(jnp.where(key_ok, score, NINF))
                    values.append(vals * mine + rest)
            tops = [jnp.max(score, axis=-1, keepdims=True) for score in scores]
            raised = [jnp.exp(score - top).astype(BF16) for score, top in zip(scores, tops)]
            parts = [dot(r, value) for r, value in zip(raised, values)]
            for i, j in enumerate(group):
                even, odd = parts[2 * i], parts[2 * i + 1]
                total = pltpu.roll(jnp.where(low, odd, even), 64, 1)
                smix[:, 128 * j:128 * j + 128] = (jnp.where(low, even, odd) / total).astype(BF16)
        done = xs[f].astype(F32) + dot(smix[...], wso[...])
        om[f] = done[0:192].astype(BF16).reshape(3, 4, 16, WIDTH)
        ol[f] = done[192:208].astype(BF16)
        pltpu.make_async_copy(om.at[f, :, me], ret.at[4 * me + f], tsnd.at[f, 0]).start()
        for k in (2, 1, 3):
            s, device = peer(k)
            remote(om.at[f, :, s], ret.at[4 * me + f], tsnd.at[f, k], trcv.at[f, k], device).start()
        return 0

    for c in range(PIECES):
        for cp in part[c] + relay[c]:
            cp.wait_send()
    for p in (0, 2, 4):
        gather(p)
    lax.fori_loop(0, 2, frame, 0)
    for p in (1, 3, 5):
        gather(p)
    lax.fori_loop(2, 4, frame, 0)
    for copies in scattered.values():
        for cp in copies:
            cp.wait_send()
    for cp in left_copies:
        cp.wait_send()

    rl[...] = dot(perm3[1], ol[...].reshape(64, WIDTH)).astype(BF16).reshape(4, 16, WIDTH)
    pltpu.make_async_copy(rl.at[me], retl.at[me], usnd.at[0]).start()
    for k in range(1, 4):
        s, device = peer(k)
        remote(rl.at[s], retl.at[me], usnd.at[k], urcv.at[k], device).start()

    for f in range(4):
        pltpu.make_async_copy(om.at[f, :, me], ret.at[4 * me + f], tsnd.at[f, 0]).wait()
        for k in (2, 1, 3):
            s, device = peer(k)
            remote(om.at[f, :, s], ret.at[4 * me + f], tsnd.at[f, k], trcv.at[f, k], device).wait()

    for c in range(CHUNKS):
        moved = dot(perm5[...], ret[:, c].reshape(256, WIDTH)).astype(BF16).reshape(16, 16, WIDTH)
        out[8 * c:8 * c + 8] = moved[0:8]
        out[25 + 8 * c:33 + 8 * c] = moved[8:16]
    pltpu.make_async_copy(rl.at[me], retl.at[me], usnd.at[0]).wait()
    for k in range(1, 4):
        s, device = peer(k)
        remote(rl.at[s], retl.at[me], usnd.at[k], urcv.at[k], device).wait()
    out[24] = (retl[0] + retl[1]) + (retl[2] + retl[3])


def on_device(frames_in, ln_time, w_time_qkv, w_time_out, ln_space, w_space_qkv, w_space_out, band_lo, band_hi, valid):
    x = jnp.transpose(frames_in, (1, 0, 2))
    any_spec = pl.BlockSpec(memory_space=pl.ANY)
    vmem_spec = pl.BlockSpec(memory_space=pltpu.VMEM)
    smem_spec = pl.BlockSpec(memory_space=pltpu.SMEM)
    dma = pltpu.SemaphoreType.DMA
    scratch = [
        pltpu.VMEM((WIDTH, 3 * WIDTH), BF16),
        pltpu.VMEM((WIDTH, WIDTH), BF16),
        pltpu.VMEM((WIDTH, 3 * WIDTH), BF16),
        pltpu.VMEM((WIDTH, WIDTH), BF16),
        pltpu.VMEM((4, HALF, BLOCK, WIDTH), BF16),
        pltpu.VMEM((288, WIDTH), BF16),
        pltpu.VMEM((4, 400, 2 * WIDTH), BF16),
        pltpu.VMEM((2, 400, WIDTH), BF16),
        pltpu.VMEM((288, WIDTH), BF16),
        pltpu.VMEM((CHUNKS, 8, 32, WIDTH), BF16),
        pltpu.VMEM((2, BLOCK, WIDTH), BF16),
        pltpu.VMEM((CHUNKS, 8, 32, WIDTH), BF16),
        pltpu.VMEM((4, BLOCK, WIDTH), BF16),
        pltpu.VMEM((4, TOKENS, WIDTH), BF16),
        pltpu.VMEM((192, WIDTH), BF16),
        pltpu.VMEM((4, TOKENS, 3 * WIDTH), BF16),
        pltpu.VMEM((TOKENS, WIDTH), BF16),
        pltpu.VMEM((4, CHUNKS, 4, BLOCK, WIDTH), BF16),
        pltpu.VMEM((4, BLOCK, WIDTH), BF16),
        pltpu.VMEM((BLOCK, CHUNKS, BLOCK, WIDTH), BF16),
        pltpu.VMEM((4, BLOCK, WIDTH), BF16),
        pltpu.VMEM((4, BLOCK, WIDTH), BF16),
        pltpu.VMEM((2, 8, 128), F32),
        pltpu.VMEM((128, 64), F32),
        pltpu.VMEM((2, 64, 64), BF16),
        pltpu.VMEM((256, 256), BF16),
        pltpu.VMEM((128, 128), BF16),
        pltpu.VMEM((256, 256), BF16),
        dma((5,)), dma((len(PARCELS) + 1,)),
        *[dma((2, PIECES))] * 4, dma((2,)),
        dma((len(PARCELS), 8)), dma((len(PARCELS), 8)), dma((4,)), dma((4,)),
        dma((4, 4)), dma((4, 4)), dma((4,)), dma((4,)),
    ]
    result = pl.pallas_call(
        kernel,
        out_shape=pltpu.VMEM((PATCH, BLOCK, WIDTH), BF16),
        in_specs=[any_spec] * 5 + [vmem_spec] * 2 + [smem_spec] * 3,
        out_specs=vmem_spec,
        scratch_shapes=scratch,
        compiler_params=pltpu.CompilerParams(
            collective_id=0, has_side_effects=True, vmem_limit_bytes=56 * 1024 * 1024
        ),
    )(
        x, w_time_qkv, w_time_out, w_space_qkv, w_space_out,
        ln_time, ln_space, band_lo, band_hi, valid,
    )
    return jnp.transpose(result, (1, 0, 2))


def solution(mesh):
    placed = (P("tm", "patch", None), P(), P(), P(), P(), P(), P(), P("tm"), P("tm"), P())
    return jax.shard_map(
        on_device, mesh=mesh, in_specs=placed, out_specs=P("tm", "patch", None), check_vma=False
    )
```

```python
import functools

import jax
import jax.numpy as jnp
from jax import lax
from jax.experimental import pallas as pl
from jax.experimental.pallas import tpu as pltpu
from jax.sharding import PartitionSpec as P

MESH = pl.DeviceIdType.MESH
F32 = jnp.float32
BF16 = jnp.bfloat16
HEADS = 12
BLOCK = 16
WIDTH = 768
PATCH = 49
HALF = 25
GROUP = 8
CHUNKS = 3
PIECES = 9
PARCELS = ((0, 0), (0, 16), (1, 0), (1, 16), (2, 0), (2, 16))
BOUNDS = (0, 1, 3, 6, 9, 13, 17, 21, 23, 25)
TOKENS = 208
VALID = 196
NT = (((1,), (1,)), ((), ()))
NINF = float("-inf")


def dot(a, b):
    return jnp.dot(a, b, preferred_element_type=F32)


def norm_rows(values, gain):
    floats = values.astype(F32)
    center = floats - jnp.mean(floats, axis=-1, keepdims=True)
    spread = jnp.mean(center * center, axis=-1, keepdims=True)
    return (center * lax.rsqrt(spread + 1e-05) * gain).astype(BF16)


def select_matrix(rows, cols, source):
    row = lax.broadcasted_iota(jnp.int32, (rows, cols), 0)
    col = lax.broadcasted_iota(jnp.int32, (rows, cols), 1)
    return jnp.where(source(row) == col, 1.0, 0.0).astype(BF16)


def bits(value, low, count):
    return (value >> low) & ((1 << count) - 1)


def kernel(
    x_hbm, wtq_hbm, wto_hbm, wsq_hbm, wso_hbm, gt_hbm, gs_hbm, band_lo, band_hi, valid_hbm, out,
    gain_t, gain_s, valid,
    wtq, wto, wsq, wso, x4, nrm, kv, qs, mix, snd, lft, recv, rcl, xs, nrm2, qkv, smix,
    om, ol, ret, rl, retl, biasb, bias, perm3, perm6, perm7, perm5,
    lsem, csem, psnd, prcv, rsnd, rrcv, bsem,
    ssnd, srcv, lsnd, lrcv, tsnd, trcv, usnd, urcv,
):
    tm = lax.axis_index("tm")
    me = lax.axis_index("patch")
    pairs = lax.axis_size("tm") // 2
    pair = tm // 2
    side = tm % 2
    own = 1 + side
    gid = side * 4 + me
    home = (me + 2) % 4
    slot_id = side * 4 + home
    partner = (pair * 2 + 1 - side, me)
    before = ((pair - 1 + pairs) % pairs * 2 + side, me)
    behind = ((pair + 1) % pairs * 2 + side, me)

    def member(k):
        d = (gid + k) % 8
        return d, (pair * 2 + d // 4, d % 4)

    def peer(k):
        s = (me + k) % 4
        return s, (tm, s)

    def remote(src, dst, snd_sem, rcv_sem, device):
        return pltpu.make_async_remote_copy(
            src_ref=src, dst_ref=dst, send_sem=snd_sem, recv_sem=rcv_sem,
            device_id=device, device_id_type=MESH,
        )

    small_copies = []
    for i, (src, dst) in enumerate(((valid_hbm, valid), (gt_hbm, gain_t), (gs_hbm, gain_s))):
        cp = pltpu.make_async_copy(src, dst, lsem.at[4 + i])
        cp.start()
        small_copies.append(cp)
    w_copies = []
    for i, (src, dst) in enumerate(((wtq_hbm, wtq), (wto_hbm, wto), (wsq_hbm, wsq), (wso_hbm, wso))):
        cp = pltpu.make_async_copy(src, dst, lsem.at[i])
        cp.start()
        w_copies.append(cp)

    barrier = pltpu.get_barrier_semaphore()
    for k in range(1, 8):
        pl.semaphore_signal(barrier, inc=1, device_id=member(k)[1], device_id_type=MESH)
    pl.semaphore_signal(barrier, inc=1, device_id=before, device_id_type=MESH)
    pl.semaphore_signal(barrier, inc=1, device_id=behind, device_id_type=MESH)
    pl.semaphore_wait(barrier, 9)

    def piece(c):
        return pl.ds(BOUNDS[c], BOUNDS[c + 1] - BOUNDS[c])

    part, relay = [], []
    for c in range(PIECES):
        lo, n = BOUNDS[c], BOUNDS[c + 1] - BOUNDS[c]
        part.append([
            remote(
                x_hbm.at[pl.ds(25 * half + lo - 1 if c else 24, n)], x4.at[own, piece(c)],
                psnd.at[half, c], prcv.at[side, c], (pair * 2 + half, home),
            )
            for half in range(2)
        ])
        relay.append([
            remote(x4.at[1, piece(c)], x4.at[3, piece(c)], rsnd.at[0, c], rrcv.at[0, c], before),
            remote(x4.at[2, piece(c)], x4.at[0, piece(c)], rsnd.at[1, c], rrcv.at[1, c], behind),
        ])
    for c in range(4):
        for cp in part[c]:
            cp.start()
    for cp in small_copies:
        cp.wait()
    lane = lax.broadcasted_iota(jnp.int32, (1, 2 * pairs), 1)
    flags = valid[...].reshape(1, 2 * pairs).astype(F32)
    left_flag = jnp.sum(jnp.where(lane == tm - 1, flags, 0.0), axis=-1, keepdims=True)
    right_flag = jnp.sum(jnp.where(lane == tm + 1, flags, 0.0), axis=-1, keepdims=True)
    left_ok = (band_lo[0] <= -1) & (left_flag == 1.0)
    right_ok = (band_hi[0] >= 1) & (right_flag == 1.0)
    row8 = lax.broadcasted_iota(jnp.int32, (8, 128), 0)
    biasb[side] = jnp.where(row8 == 0, jnp.where(left_ok, 0.0, NINF), jnp.where(right_ok, 0.0, NINF))
    bias_copy = remote(biasb.at[side], biasb.at[side], bsem.at[0], bsem.at[1], partner)
    bias_copy.start()
    for c in range(4, PIECES):
        for cp in part[c]:
            cp.start()

    perm6[...] = select_matrix(
        256, 256,
        lambda r: (bits(r, 7, 1) << 7) | (bits(r, 1, 3) << 4) | (bits(r, 5, 2) << 2)
        | (bits(r, 4, 1) << 1) | bits(r, 0, 1),
    )
    perm7[...] = select_matrix(
        128, 128, lambda r: (bits(r, 3, 1) << 6) | (bits(r, 4, 2) << 4) | (bits(r, 0, 3) << 1) | bits(r, 6, 1)
    )
    perm5[...] = select_matrix(256, 256, lambda r: (bits(r, 0, 4) << 4) | bits(r, 4, 4))
    perm3[0] = select_matrix(
        64, 64, lambda r: jnp.where(bits(r, 0, 4) < 4, (bits(r, 0, 2) << 4) + me * 4 + bits(r, 4, 2), -1)
    )
    perm3[1] = select_matrix(
        64, 64, lambda r: jnp.where(bits(r, 2, 2) == me, (bits(r, 0, 2) << 4) + bits(r, 4, 2), -1)
    )

    lane256 = lax.broadcasted_iota(jnp.int32, (1, 256), 1) >> 6
    head_f = [lane256 == h for h in range(4)]
    head_b = [jnp.where(m, 1.0, 0.0).astype(BF16) for m in head_f]

    def project(slots, lo, n, queries):
        rows = 16 * n
        for i, slot in enumerate(slots):
            block = x4[slot, lo:lo + n].reshape(rows, WIDTH)
            nrm[rows * i:rows * i + rows] = norm_rows(block, gain_t[...].reshape(1, WIDTH))
        normed = nrm[0:rows * len(slots)]
        pairs_kv = dot(normed, wtq[:, WIDTH:]).astype(BF16)
        for i, slot in enumerate(slots):
            kv[slot, 16 * lo:16 * lo + rows] = pairs_kv[rows * i:rows * i + rows]
        if queries:
            query = dot(normed, wtq[:, 0:WIDTH]).astype(BF16) * jnp.asarray(0.125, BF16)
            for i in range(2):
                qs[i, 16 * lo:16 * lo + rows] = query[rows * i:rows * i + rows]

    def attend(places):
        scores, values = [], []
        for at, _ in places:
            q_all = [qs[b, at:at + 16] for b in range(2)]
            for g in range(3):
                cols = slice(256 * g, 256 * g + 256)
                vcols = slice(768 + 256 * g, 768 + 256 * g + 256)
                keys = jnp.concatenate([kv[slot, at:at + 16, cols] for slot in range(4)], axis=0)
                values.append(jnp.concatenate([kv[slot, at:at + 16, vcols] for slot in range(4)], axis=0))
                query = jnp.concatenate([q[:, cols] for q in q_all], axis=0)
                stacked = jnp.concatenate([query * m for m in head_b], axis=0)
                scores.append(lax.dot_general(stacked, keys, NT, preferred_element_type=F32) + bias[...])
        tops = [jnp.max(score, axis=-1, keepdims=True) for score in scores]
        raised = [jnp.exp(score - top) for score, top in zip(scores, tops)]
        scales = [1.0 / jnp.sum(r, axis=-1, keepdims=True) for r in raised]
        weights = [(r * scale).astype(BF16) for r, scale in zip(raised, scales)]
        mixed = [dot(weight, value) for weight, value in zip(weights, values)]
        for i, part_mix in enumerate(mixed):
            rows, cols = places[i // 3][1], slice(256 * (i % 3), 256 * (i % 3) + 256)
            picked = jnp.where(head_f[0], part_mix[0:32], 0.0)
            for h in range(1, 4):
                picked = jnp.where(head_f[h], part_mix[32 * h:32 * h + 32], picked)
            picked = picked.astype(BF16)
            mix[rows[0]:rows[0] + 16, cols] = picked[:16]
            mix[rows[1]:rows[1] + 16, cols] = picked[16:]

    def mix_unit(u):
        places = [(16 * (1 + GROUP * u + j), (16 * j, 128 + 16 * j)) for j in range(GROUP)]
        attend(places + [(0, (256, 272))] if u == 0 else places)

    def send_unit(u):
        first = 1 + GROUP * u
        acc = dot(mix[0:288 if u == 0 else 256], wto[...])
        base = x4[1:3, first:first + GROUP].reshape(256, WIDTH)
        after = (base.astype(F32) + acc[0:256]).astype(BF16)
        snd[u] = dot(perm6[...], after).astype(BF16).reshape(8, 32, WIDTH)
        if u == 0:
            base = x4[1:3, 0].reshape(32, WIDTH)
            lft[...] = (base.astype(F32) + acc[256:288]).astype(BF16).reshape(2, 16, WIDTH)
        scatter(2 * u)

    def own_piece(p):
        c, at = PARCELS[p]
        rows = pl.ds(at, 16)
        return pltpu.make_async_copy(snd.at[c, gid, rows], recv.at[c, slot_id, rows], csem.at[p])

    scattered = {}

    def scatter(p):
        c, at = PARCELS[p]
        rows = pl.ds(at, 16)
        scattered[p] = []
        own_piece(p).start()
        for k in (2, 6, 4, 3, 5, 1, 7):
            d, device = member(k)
            cp = remote(snd.at[c, d, rows], recv.at[c, slot_id, rows], ssnd.at[p, k], srcv.at[p, k], device)
            cp.start()
            scattered[p].append(cp)

    def span(first, count):
        return BOUNDS[first], BOUNDS[first + count] - BOUNDS[first]

    bias_copy.wait()
    key_slot = lax.broadcasted_iota(jnp.int32, (32, 64), 1) >> 4
    query_blk = lax.broadcasted_iota(jnp.int32, (32, 64), 0) >> 4
    offset = key_slot - 1 - query_blk
    one = jnp.where(
        query_blk == 0,
        jnp.where(offset < 0, biasb[0, 0:1, 0:64], biasb[0, 1:2, 0:64]),
        jnp.where(offset < 0, biasb[1, 0:1, 0:64], biasb[1, 1:2, 0:64]),
    )
    one = jnp.where(offset == 0, 0.0, one)
    one = jnp.where((offset > 1) | (offset < -1), NINF, one)
    for h in range(4):
        bias[32 * h:32 * h + 32] = one

    w_copies[0].wait()
    w_copies[1].wait()

    def forward(c):
        for b in range(2):
            remote(
                x4.at[1 + b, piece(c)], x4.at[1 + b, piece(c)], psnd.at[b, c], prcv.at[b, c], partner
            ).wait_recv()
            relay[c][b].start()

    def mine(*pieces):
        project((1, 2), *span(pieces[0], len(pieces)), True)

    def halos(*pieces):
        for c in pieces:
            for cp in relay[c]:
                cp.wait_recv()

    def beside(*pieces):
        project((0, 3), *span(pieces[0], len(pieces)), False)

    for c in range(4):
        forward(c)
    mine(0, 1, 2, 3)
    forward(4)
    mine(4)
    halos(0, 1, 2, 3)
    forward(5)
    beside(0, 1, 2, 3)
    mix_unit(0)
    forward(6)
    send_unit(0)
    left_copies = []
    pltpu.make_async_copy(lft.at[side], rcl.at[home], csem.at[len(PARCELS)]).start()
    for k in range(1, 4):
        s, device = peer(k)
        cp = remote(lft.at[side], rcl.at[home], lsnd.at[k], lrcv.at[k], device)
        cp.start()
        left_copies.append(cp)
    forward(7)
    mine(5, 6)
    forward(8)
    halos(4, 5)
    beside(4, 5)
    mix_unit(1)
    send_unit(1)
    mine(7, 8)
    halos(6, 7, 8)
    beside(6, 7, 8)
    mix_unit(2)
    send_unit(2)
    for p in (1, 3, 5):
        scatter(p)
    w_copies[2].wait()
    w_copies[3].wait()

    def gather(p):
        c, first = PARCELS[p]
        last, at = p == 0, 64 * c
        frames = slice(first // 8, first // 8 + 2)
        own_piece(p).wait()
        for cp in scattered[p]:
            cp.wait_recv()
        moved = dot(perm7[...], recv[c, :, first:first + 16].reshape(128, WIDTH)).astype(BF16)
        xs[frames, at:at + 64] = moved.reshape(2, 64, WIDTH)
        nrm2[0:128] = norm_rows(moved, gain_s[...].reshape(1, WIDTH))
        total = 128
        if last:
            pltpu.make_async_copy(lft.at[side], rcl.at[home], csem.at[len(PARCELS)]).wait()
            for cp in left_copies:
                cp.wait_recv()
            moved = dot(perm3[0], rcl[...].reshape(64, WIDTH)).astype(BF16)
            xs[:, 192:208] = moved.reshape(4, 16, WIDTH)
            nrm2[128:192] = norm_rows(moved, gain_s[...].reshape(1, WIDTH))
            total = 192
        for j in range(3):
            cols = slice(WIDTH * j, WIDTH * j + WIDTH)
            tile = dot(nrm2[0:total], wsq[:, cols]).astype(BF16)
            if j == 0:
                tile = tile * jnp.asarray(0.125, BF16)
            qkv[frames, at:at + 64, cols] = tile[0:128].reshape(2, 64, WIDTH)
            if last:
                qkv[:, 192:208, cols] = tile[128:192].reshape(4, 16, WIDTH)

    lane128 = lax.broadcasted_iota(jnp.int32, (1, 128), 1)
    low = lane128 < 64
    low_b = jnp.where(low, 1.0, 0.0).astype(BF16)
    high_b = jnp.where(low, 0.0, 1.0).astype(BF16)
    key_ok = lax.broadcasted_iota(jnp.int32, (1, TOKENS), 1) < VALID

    def frame(f, _):
        for first in (0, 3):
            group = range(first, first + 3)
            scores, values = [], []
            for j in group:
                query = qkv[f, :, 128 * j:128 * j + 128]
                keys = qkv[f, :, WIDTH + 128 * j:WIDTH + 128 * j + 128]
                vals = qkv[f, :, 2 * WIDTH + 128 * j:2 * WIDTH + 128 * j + 128]
                for mine, rest in ((low_b, high_b), (high_b, low_b)):
                    score = lax.dot_general(query * mine, keys, NT, preferred_element_type=F32)
                    scores.append(jnp.where(key_ok, score, NINF))
                    values.append(vals * mine + rest)
            tops = [jnp.max(score, axis=-1, keepdims=True) for score in scores]
            raised = [jnp.exp(score - top).astype(BF16) for score, top in zip(scores, tops)]
            parts = [dot(r, value) for r, value in zip(raised, values)]
            for i, j in enumerate(group):
                even, odd = parts[2 * i], parts[2 * i + 1]
                total = pltpu.roll(jnp.where(low, odd, even), 64, 1)
                smix[:, 128 * j:128 * j + 128] = (jnp.where(low, even, odd) / total).astype(BF16)
        done = xs[f].astype(F32) + dot(smix[...], wso[...])
        om[f] = done[0:192].astype(BF16).reshape(3, 4, 16, WIDTH)
        ol[f] = done[192:208].astype(BF16)
        pltpu.make_async_copy(om.at[f, :, me], ret.at[4 * me + f], tsnd.at[f, 0]).start()
        for k in (2, 1, 3):
            s, device = peer(k)
            remote(om.at[f, :, s], ret.at[4 * me + f], tsnd.at[f, k], trcv.at[f, k], device).start()
        return 0

    for c in range(PIECES):
        for cp in part[c] + relay[c]:
            cp.wait_send()
    for p in (0, 2, 4):
        gather(p)
    lax.fori_loop(0, 2, frame, 0)
    for p in (1, 3, 5):
        gather(p)
    lax.fori_loop(2, 4, frame, 0)
    for copies in scattered.values():
        for cp in copies:
            cp.wait_send()
    for cp in left_copies:
        cp.wait_send()

    rl[...] = dot(perm3[1], ol[...].reshape(64, WIDTH)).astype(BF16).reshape(4, 16, WIDTH)
    pltpu.make_async_copy(rl.at[me], retl.at[me], usnd.at[0]).start()
    for k in range(1, 4):
        s, device = peer(k)
        remote(rl.at[s], retl.at[me], usnd.at[k], urcv.at[k], device).start()

    for f in range(4):
        pltpu.make_async_copy(om.at[f, :, me], ret.at[4 * me + f], tsnd.at[f, 0]).wait()
        for k in (2, 1, 3):
            s, device = peer(k)
            remote(om.at[f, :, s], ret.at[4 * me + f], tsnd.at[f, k], trcv.at[f, k], device).wait()

    for c in range(CHUNKS):
        moved = dot(perm5[...], ret[:, c].reshape(256, WIDTH)).astype(BF16).reshape(16, 16, WIDTH)
        out[8 * c:8 * c + 8] = moved[0:8]
        out[25 + 8 * c:33 + 8 * c] = moved[8:16]
    pltpu.make_async_copy(rl.at[me], retl.at[me], usnd.at[0]).wait()
    for k in range(1, 4):
        s, device = peer(k)
        remote(rl.at[s], retl.at[me], usnd.at[k], urcv.at[k], device).wait()
    out[24] = (retl[0] + retl[1]) + (retl[2] + retl[3])


def on_device(frames_in, ln_time, w_time_qkv, w_time_out, ln_space, w_space_qkv, w_space_out, band_lo, band_hi, valid):
    x = jnp.transpose(frames_in, (1, 0, 2))
    any_spec = pl.BlockSpec(memory_space=pl.ANY)
    smem_spec = pl.BlockSpec(memory_space=pltpu.SMEM)
    vmem_spec = pl.BlockSpec(memory_space=pltpu.VMEM)
    dma = pltpu.SemaphoreType.DMA
    scratch = [
        pltpu.VMEM((WIDTH,), F32),
        pltpu.VMEM((WIDTH,), F32),
        pltpu.VMEM(valid.shape, jnp.int32),
        pltpu.VMEM((WIDTH, 3 * WIDTH), BF16),
        pltpu.VMEM((WIDTH, WIDTH), BF16),
        pltpu.VMEM((WIDTH, 3 * WIDTH), BF16),
        pltpu.VMEM((WIDTH, WIDTH), BF16),
        pltpu.VMEM((4, HALF, BLOCK, WIDTH), BF16),
        pltpu.VMEM((288, WIDTH), BF16),
        pltpu.VMEM((4, 400, 2 * WIDTH), BF16),
        pltpu.VMEM((2, 400, WIDTH), BF16),
        pltpu.VMEM((288, WIDTH), BF16),
        pltpu.VMEM((CHUNKS, 8, 32, WIDTH), BF16),
        pltpu.VMEM((2, BLOCK, WIDTH), BF16),
        pltpu.VMEM((CHUNKS, 8, 32, WIDTH), BF16),
        pltpu.VMEM((4, BLOCK, WIDTH), BF16),
        pltpu.VMEM((4, TOKENS, WIDTH), BF16),
        pltpu.VMEM((192, WIDTH), BF16),
        pltpu.VMEM((4, TOKENS, 3 * WIDTH), BF16),
        pltpu.VMEM((TOKENS, WIDTH), BF16),
        pltpu.VMEM((4, CHUNKS, 4, BLOCK, WIDTH), BF16),
        pltpu.VMEM((4, BLOCK, WIDTH), BF16),
        pltpu.VMEM((BLOCK, CHUNKS, BLOCK, WIDTH), BF16),
        pltpu.VMEM((4, BLOCK, WIDTH), BF16),
        pltpu.VMEM((4, BLOCK, WIDTH), BF16),
        pltpu.VMEM((2, 8, 128), F32),
        pltpu.VMEM((128, 64), F32),
        pltpu.VMEM((2, 64, 64), BF16),
        pltpu.VMEM((256, 256), BF16),
        pltpu.VMEM((128, 128), BF16),
        pltpu.VMEM((256, 256), BF16),
        dma((7,)), dma((len(PARCELS) + 1,)),
        *[dma((2, PIECES))] * 4, dma((2,)),
        dma((len(PARCELS), 8)), dma((len(PARCELS), 8)), dma((4,)), dma((4,)),
        dma((4, 4)), dma((4, 4)), dma((4,)), dma((4,)),
    ]
    result = pl.pallas_call(
        kernel,
        out_shape=pltpu.VMEM((PATCH, BLOCK, WIDTH), BF16),
        in_specs=[any_spec] * 7 + [smem_spec] * 2 + [any_spec],
        out_specs=vmem_spec,
        scratch_shapes=scratch,
        compiler_params=pltpu.CompilerParams(
            collective_id=0, has_side_effects=True, vmem_limit_bytes=56 * 1024 * 1024
        ),
    )(
        x, w_time_qkv, w_time_out, w_space_qkv, w_space_out,
        ln_time, ln_space, band_lo, band_hi, valid,
    )
    return jnp.transpose(result, (1, 0, 2))


def solution(mesh):
    placed = (P("tm", "patch", None), P(), P(), P(), P(), P(), P(), P("tm"), P("tm"), P())
    return jax.shard_map(
        on_device, mesh=mesh, in_specs=placed, out_specs=P("tm", "patch", None), check_vma=False
    )
```
